512 devices in a mesh: section: 16 (over x, y_lo, core), bulk: 32 (over y_hi, z).
Axes of the slice: x: 4, y: 8 (y_hi: 4, y_lo: 2; y = y_hi * 2 + y_lo), z: 8, core: 2. Of those that a mesh axis runs over, the one named last changes fastest.
Arguments:
- activations: bfloat16 [16, 4, 8192, 256], P('section', None, 'bulk'), may hold values from -6 to 6
- weights: bfloat16 [16, 3, 256, 256], P('section'), may hold values from -0.109375 to 0.109375
- film_gain: float32 [16, 36, 256], P('section'), may hold values from 0.25 to 1.75
- film_shift: float32 [16, 36, 256], P('section'), may hold values from -3 to 3
- doa_bins: int32 [4], replicated, may hold values from 0 to 35
- cotangent: bfloat16 [4, 8192, 256], P(None, 'bulk'), may hold values from -6 to 6
Outputs:
- d_inputs: bfloat16 [16, 4, 8192, 256], P('section', None, 'bulk')
- d_weights: float32 [16, 3, 256, 256], P('section')
- d_gain: float32 [16, 36, 256], P('section')
- d_shift: float32 [16, 36, 256], P('section')
The draws below stay inside these ranges and needn't reach their ends.
All inputs are finite; a program needn't handle non-finite values.
Results may differ from the reference program's by a relative error of at most 0.014.
Values may be sent and summed in bfloat16 or wider, within the bound.
A program may use at most 64 MiB of HBM per device.

```python
import jax
import jax.numpy as jnp

C = 256
BINS = 36
MB = 4
PIX = 8192
SECTIONS = 16


def with_ends(values, rng, smallest, largest):
    longest = values.shape.index(max(values.shape))
    spots = []
    for shift in (0, 1):
        where = [jax.random.randint(jax.random.fold_in(rng, axis), (), 0, length) for axis, length in enumerate(values.shape)]
        where[longest] = (where[longest] + shift) % values.shape[longest]
        spots.append(tuple(where))
    return values.at[spots[0]].set(smallest).at[spots[1]].set(largest)


def block_scale(rng, dims, cuts, low, top_value):
    def one(axis_at, blocks):
        draws = jax.random.uniform(jax.random.fold_in(jax.random.fold_in(rng, 6), axis_at), (blocks,), jnp.float32, low / len(cuts), top_value / len(cuts))
        return jnp.repeat(jnp.exp(draws), dims[axis_at] // blocks).reshape((-1,) + (1,) * (len(dims) - axis_at - 1))

    gain = one(*cuts[0])
    for cut in cuts[1:]:
        gain = gain * one(*cut)
    return gain


def normal_values(key, dims, deviation, bound, cuts=(), held_as=jnp.bfloat16):
    loudness = block_scale(key, dims, cuts, -0.22, 0.18) if cuts else 1.0
    entries = jax.random.normal(key, dims, jnp.float32) * deviation * loudness
    return jnp.minimum(jnp.maximum(entries, -bound), bound).astype(held_as)


def setup_inputs(seed: int = 0) -> dict:
    arg_keys = jax.random.split(jax.random.key(seed), 7)
    return {
        "activations": normal_values(arg_keys[0], (SECTIONS, MB, PIX, C), 1.0, 6.0, ((0, 16), (2, 32))),
        "weights": normal_values(arg_keys[1], (SECTIONS, 3, C, C), (12 * C) ** -0.5, 0.109375, ((0, 16),)),
        "film_gain": jnp.clip(1.0 + 0.15 * jax.random.normal(arg_keys[2], (SECTIONS, BINS, C), jnp.float32), 0.25, 1.75),
        "film_shift": normal_values(arg_keys[3], (SECTIONS, BINS, C), 0.5, 3.0, ((0, 16),), jnp.float32),
        "doa_bins": with_ends(jax.random.randint(arg_keys[4], (MB,), 0, BINS), jax.random.fold_in(arg_keys[4], 1), 0, BINS - 1).astype(jnp.int32),
        "cotangent": normal_values(arg_keys[5], (MB, PIX, C), 1.0, 6.0, ((1, 32),)),
    }


def reference(activations, weights, film_gain, film_shift, doa_bins, cotangent):
    section_total = activations.shape[0]
    micro_count = activations.shape[1]
    channels = activations.shape[3]
    bins_count = film_gain.shape[1]
    grads = [cotangent[batch_no] for batch_no in range(micro_count)]
    section_inputs = [None] * section_total
    section_weights = [None] * section_total
    section_gains = [None] * section_total
    section_shifts = [None] * section_total
    for section_no in range(section_total - 1, -1, -1):
        w_set = weights[section_no]
        grad_w = jnp.zeros((3, channels, channels), jnp.float32)
        grad_gain = jnp.zeros((bins_count, channels), jnp.float32)
        grad_shift = jnp.zeros((bins_count, channels), jnp.float32)
        for batch_no in range(micro_count):
            act_now = activations[section_no, batch_no]
            before = jnp.roll(act_now, 1, 0)
            after = jnp.roll(act_now, -1, 0)
            pre_film = jnp.dot(before, w_set[0], preferred_element_type=jnp.float32)
            pre_film = pre_film + jnp.dot(act_now, w_set[1], preferred_element_type=jnp.float32)
            pre_film = pre_film + jnp.dot(after, w_set[2], preferred_element_type=jnp.float32)
            bin_id = doa_bins[batch_no]
            gain_row = film_gain[section_no, bin_id]
            shift_row = film_shift[section_no, bin_id]
            filmed = pre_film * gain_row + shift_row
            sigmoid_v = jax.nn.sigmoid(filmed)
            top_grad = grads[batch_no].astype(jnp.float32)
            grad_film = top_grad * sigmoid_v * (1.0 + filmed * (1.0 - sigmoid_v))
            grad_pre = (grad_film * gain_row).astype(jnp.bfloat16)
            back_prev = jnp.dot(grad_pre, w_set[0].T, preferred_element_type=jnp.float32)
            back_mid = jnp.dot(grad_pre, w_set[1].T, preferred_element_type=jnp.float32)
            back_next = jnp.dot(grad_pre, w_set[2].T, preferred_element_type=jnp.float32)
            grad_input = top_grad + jnp.roll(back_prev, -1, 0) + back_mid + jnp.roll(back_next, 1, 0)
            grads[batch_no] = grad_input.astype(jnp.bfloat16)
            grad_w = grad_w + jnp.stack([
                jnp.dot(before.T, grad_pre, preferred_element_type=jnp.float32),
                jnp.dot(act_now.T, grad_pre, preferred_element_type=jnp.float32),
                jnp.dot(after.T, grad_pre, preferred_element_type=jnp.float32)])
            grad_gain = grad_gain.at[bin_id].add(jnp.sum(grad_film * pre_film, 0))
            grad_shift = grad_shift.at[bin_id].add(jnp.sum(grad_film, 0))
        section_inputs[section_no] = jnp.stack(grads)
        section_weights[section_no] = grad_w
        section_gains[section_no] = grad_gain
        section_shifts[section_no] = grad_shift
    return (jnp.stack(section_inputs), jnp.stack(section_weights), jnp.stack(section_gains), jnp.stack(section_shifts))
```

```python
import functools

import jax
import jax.numpy as jnp
from jax import lax
from jax.experimental import pallas as pl
from jax.experimental.pallas import tpu as pltpu
from jax.sharding import PartitionSpec as P

MESH = pl.DeviceIdType.MESH
F32 = jnp.float32
BF16 = jnp.bfloat16


def rolled(value, shift):
    return pltpu.roll(value, shift % value.shape[0], 0)


def body(sizes, x_ref, w_ref, gain_ref, shift_ref, bins_ref, cot_ref,
         din_ref, dw_ref, dgain_ref, dshift_ref,
         xh, wt, xt, gbuf, obuf, gpre, dgrad, dfull, dpre, acc, small,
         wpart, wland, wsum, wgather, sland, ssum,
         hx_s, hx_r, hc_s, hc_r, ch_s, ch_r, z_s, z_r, zs_s, zs_r, y_s, y_r, ys_s, ys_r, ag_s, ag_r):
    sections, nz, ny, micro, rows, channels, halo = sizes
    bulk = nz * ny
    ext = rows + 2 * halo
    wide = 2 * halo
    blk = 3 * channels // nz
    s = lax.axis_index("section")
    b = lax.axis_index("bulk")
    z = lax.rem(b, nz)
    y = b // nz
    left = lax.rem(b + bulk - 1, bulk)
    right = lax.rem(b + 1, bulk)
    is_last = s == sections - 1

    def z_peer(k):
        return y * nz + lax.rem(z + k, nz)

    def y_peer(k):
        return lax.rem(y + k, ny) * nz + z

    barrier = pltpu.get_barrier_semaphore()

    def greet(sec, blk_id):
        pl.semaphore_signal(barrier, inc=1, device_id=(sec, blk_id), device_id_type=MESH)

    greet(s, left)
    greet(s, right)
    for k in range(1, nz):
        greet(s, z_peer(k))
    for k in range(1, ny):
        greet(s, y_peer(k))

    @pl.when(s > 0)
    def _():
        greet(s - 1, b)

    @pl.when(s < sections - 1)
    def _():
        greet(s + 1, b)

    for k in range(3):
        wt[k] = w_ref[0, k].astype(F32).T.astype(BF16)
    for m in range(micro):
        xh[m, wide:wide + rows] = x_ref[0, m]

    @pl.when(is_last)
    def _():
        for m in range(micro):
            gbuf[m, halo:halo + rows] = cot_ref[m]

    base = 2 + (nz - 1) + (ny - 1)

    chain_peers = jnp.where(s > 0, 1, 0) + jnp.where(is_last, 0, 1)
    pl.semaphore_wait(barrier, base + chain_peers)

    def copy(src, dst, send, recv, to):
        return pltpu.make_async_remote_copy(src_ref=src, dst_ref=dst, send_sem=send, recv_sem=recv, device_id=to, device_id_type=MESH)

    x_right = copy(x_ref.at[0, :, pl.ds(rows - wide, wide)], xh.at[:, pl.ds(0, wide)], hx_s.at[0], hx_r.at[0], (s, right))
    x_left = copy(x_ref.at[0, :, pl.ds(0, wide)], xh.at[:, pl.ds(wide + rows, wide)], hx_s.at[1], hx_r.at[1], (s, left))
    c_right = copy(cot_ref.at[:, pl.ds(rows - halo, halo)], gbuf.at[:, pl.ds(0, halo)], hc_s.at[0], hc_r.at[0], (s, right))
    c_left = copy(cot_ref.at[:, pl.ds(0, halo)], gbuf.at[:, pl.ds(halo + rows, halo)], hc_s.at[1], hc_r.at[1], (s, left))
    x_right.start()
    x_left.start()

    @pl.when(is_last)
    def _():
        c_right.start()
        c_left.start()

    x_right.wait()
    x_left.wait()

    def forward(m, carry):
        xs = xh[m]
        pre = rolled(jnp.dot(xs, w_ref[0, 0], preferred_element_type=F32), 1)
        pre = pre + jnp.dot(xs, w_ref[0, 1], preferred_element_type=F32)
        pre = pre + rolled(jnp.dot(xs, w_ref[0, 2], preferred_element_type=F32), -1)
        pre = pre[halo:halo + ext]
        k = bins_ref[m]
        gain = gain_ref[0, pl.ds(k, 1), :]
        filmed = pre * gain + shift_ref[0, pl.ds(k, 1), :]
        sig = jax.nn.sigmoid(filmed)
        d = sig * (1.0 + filmed * (1.0 - sig))
        dfull[m] = d * gain
        d = d[halo:halo + rows]
        dgrad[m] = d
        dpre[m] = d * pre[halo:halo + rows]
        return carry

    lax.fori_loop(0, micro, forward, 0)

    def turn(m, carry):
        xs = xh[m].astype(F32)
        for j, sh in enumerate((1, 0, -1)):
            part = rolled(xs, sh) if sh else xs
            xt[m, j * channels:(j + 1) * channels] = part[wide:wide + rows].T.astype(BF16)
        return carry

    acc[...] = jnp.zeros_like(acc)

    def weight_step(m, carry):
        acc[...] += jnp.dot(xt[m], gpre[m, halo:halo + rows], preferred_element_type=F32)
        g = gbuf[m, halo:halo + rows].astype(F32)
        small[0, pl.ds(m, 1)] = jnp.sum(g * dpre[m], 0, keepdims=True)
        small[0, pl.ds(micro + m, 1)] = jnp.sum(g * dgrad[m], 0, keepdims=True)
        return carry

    @pl.when(jnp.logical_not(is_last))
    def _():
        lax.fori_loop(0, micro, turn, 0)

    @pl.when(is_last)
    def _():
        c_right.wait()
        c_left.wait()

    def chain_copy(m):
        return copy(obuf.at[m], gbuf.at[m], ch_s.at[m], ch_r.at[m], (s - 1, b))

    def chain(m, carry):
        @pl.when(jnp.logical_not(is_last))
        def _():
            chain_copy(m).wait_recv()

        g = gbuf[m].astype(F32)
        gp = (g * dfull[m]).astype(BF16)
        gpre[m] = gp
        out = g + jnp.dot(gp, wt[1], preferred_element_type=F32)
        out = out + rolled(jnp.dot(gp, wt[0], preferred_element_type=F32), -1)
        out = out + rolled(jnp.dot(gp, wt[2], preferred_element_type=F32), 1)
        obuf[m] = out.astype(BF16)

        @pl.when(s > 0)
        def _():
            chain_copy(m).start()

        @pl.when(jnp.logical_not(is_last))
        def _():
            weight_step(m, 0)

        return carry

    lax.fori_loop(0, micro, chain, 0)

    @pl.when(is_last)
    def _():
        lax.fori_loop(0, micro, turn, 0)
        lax.fori_loop(0, micro, weight_step, 0)

    for j in range(nz):
        wpart[j] = acc[j * blk:(j + 1) * blk].astype(BF16)

    def scatter(k):
        to = lax.rem(z + k, nz)
        return copy(wpart.at[to], wland.at[k], z_s.at[k], z_r.at[k], (s, y * nz + to))

    def small_z(k):
        return copy(small.at[0], sland.at[k], zs_s.at[k], zs_r.at[k], (s, z_peer(k)))

    for k in range(1, nz):
        scatter(k).start()
        small_z(k).start()

    for m in range(micro):
        din_ref[0, m] = obuf[m, halo:halo + rows]

    total = wpart[z].astype(F32)
    for k in range(1, nz):
        scatter(k).wait_recv()
        total = total + wland[k].astype(F32)
    wsum[y] = total.astype(BF16)

    def across(k):
        return copy(wsum.at[y], wsum.at[y], y_s.at[k], y_r.at[k], (s, y_peer(k)))

    for k in range(1, ny):
        across(k).start()

    sland[0] = small[0]
    for k in range(1, nz):
        small_z(k).wait_recv()
    tiny = sland[lax.rem(z, nz)]
    for j in range(1, nz):
        tiny = tiny + sland[lax.rem(z + nz - j, nz)]
    ssum[y] = tiny

    def small_y(k):
        return copy(ssum.at[y], ssum.at[y], ys_s.at[k], ys_r.at[k], (s, y_peer(k)))

    for k in range(1, ny):
        small_y(k).start()

    for k in range(1, ny):
        across(k).wait_recv()
    total = wsum[0].astype(F32)
    for j in range(1, ny):
        total = total + wsum[j].astype(F32)
    wgather[z] = total.astype(BF16)

    def gather(k):
        return copy(wgather.at[z], wgather.at[z], ag_s.at[k], ag_r.at[k], (s, z_peer(k)))

    for k in range(1, nz):
        gather(k).start()

    for k in range(1, ny):
        small_y(k).wait_recv()
    tiny = ssum[0]
    for j in range(1, ny):
        tiny = tiny + ssum[j]
    bins_count = dgain_ref.shape[1]
    spot = lax.broadcasted_iota(jnp.int32, (bins_count, channels), 0)
    out_gain = jnp.zeros((bins_count, channels), F32)
    out_shift = jnp.zeros((bins_count, channels), F32)
    for m in range(micro):
        hit = spot == bins_ref[m]
        out_gain = out_gain + jnp.where(hit, tiny[m:m + 1], 0.0)
        out_shift = out_shift + jnp.where(hit, tiny[micro + m:micro + m + 1], 0.0)
    dgain_ref[0] = out_gain
    dshift_ref[0] = out_shift

    for k in range(1, nz):
        gather(k).wait_recv()
    for j in range(nz):
        dw_ref[0, j * blk:(j + 1) * blk] = wgather[j].astype(F32)

    for k in range(1, nz):
        scatter(k).wait_send()
        small_z(k).wait_send()
        gather(k).wait_send()
    for k in range(1, ny):
        across(k).wait_send()
        small_y(k).wait_send()

    @pl.when(s > 0)
    def _():
        for m in range(micro):
            chain_copy(m).wait_send()


def shards(sections, bulk, activations, weights, film_gain, film_shift, doa_bins, cotangent):
    micro, rows, channels = activations.shape[1:]
    bins_count = film_gain.shape[1]
    nz = 8 if bulk == 32 else 2
    ny = bulk // nz
    halo = 16
    ext = rows + 2 * halo
    blk = 3 * channels // nz
    sizes = (sections, nz, ny, micro, rows, channels, halo)
    dma = pltpu.SemaphoreType.DMA
    vmem = pl.BlockSpec(memory_space=pltpu.VMEM)
    outs = pl.pallas_call(
        functools.partial(body, sizes),
        out_shape=(
            jax.ShapeDtypeStruct((1, micro, rows, channels), BF16),
            jax.ShapeDtypeStruct((1, 3 * channels, channels), F32),
            jax.ShapeDtypeStruct((1, bins_count, channels), F32),
            jax.ShapeDtypeStruct((1, bins_count, channels), F32),
        ),
        in_specs=[vmem, vmem, vmem, vmem, pl.BlockSpec(memory_space=pltpu.SMEM), vmem],
        out_specs=(vmem, vmem, vmem, vmem),
        scratch_shapes=[
            pltpu.VMEM((micro, ext + 2 * halo, channels), BF16),
            pltpu.VMEM((3, channels, channels), BF16),
            pltpu.VMEM((micro, 3 * channels, rows), BF16),
            pltpu.VMEM((micro, ext, channels), BF16),
            pltpu.VMEM((micro, ext, channels), BF16),
            pltpu.VMEM((micro, ext, channels), BF16),
            pltpu.VMEM((micro, rows, channels), F32),
            pltpu.VMEM((micro, ext, channels), F32),
            pltpu.VMEM((micro, rows, channels), F32),
            pltpu.VMEM((3 * channels, channels), F32),
            pltpu.VMEM((1, 2 * micro, channels), F32),
            pltpu.VMEM((nz, blk, channels), BF16),
            pltpu.VMEM((nz, blk, channels), BF16),
            pltpu.VMEM((ny, blk, channels), BF16),
            pltpu.VMEM((nz, blk, channels), BF16),
            pltpu.VMEM((nz, 2 * micro, channels), F32),
            pltpu.VMEM((ny, 2 * micro, channels), F32),
            dma((2,)), dma((2,)), dma((2,)), dma((2,)), dma((micro,)), dma((micro,)),
            dma((nz,)), dma((nz,)), dma((nz,)), dma((nz,)), dma((ny,)), dma((ny,)), dma((ny,)), dma((ny,)),
            dma((nz,)), dma((nz,)),
        ],
        compiler_params=pltpu.CompilerParams(
            collective_id=0, has_side_effects=True, vmem_limit_bytes=48 * 1024 * 1024
        ),
    )(activations, weights, film_gain, film_shift, doa_bins, cotangent)
    d_in, d_w, d_gain, d_shift = outs
    return d_in, d_w.reshape(1, 3, channels, channels), d_gain, d_shift


def solution(mesh):
    return jax.shard_map(
        functools.partial(shards, mesh.shape["section"], mesh.shape["bulk"]),
        mesh=mesh,
        in_specs=(
            P("section", None, "bulk", None),
            P("section", None, None, None),
            P("section", None, None),
            P("section", None, None),
            P(),
            P(None, "bulk", None),
        ),
        out_specs=(
            P("section", None, "bulk", None),
            P("section", None, None, None),
            P("section", None, None),
            P("section", None, None),
        ),
        check_vma=False,
    )
```

```python
import functools

import jax
import jax.numpy as jnp
from jax import lax
from jax.experimental import pallas as pl
from jax.experimental.pallas import tpu as pltpu
from jax.sharding import PartitionSpec as P

MESH = pl.DeviceIdType.MESH
F32 = jnp.float32
BF16 = jnp.bfloat16
HALO = 16
PARTS = 2


def rolled(value, shift):
    return pltpu.roll(value, shift % value.shape[0], 0)


def dot(left, right):
    return jnp.dot(left, right, preferred_element_type=F32)


def chain_body(sizes, x_ref, w_ref, gain_ref, shift_ref, bins_ref, cot_ref,
               din_ref, wgather, tiny_ref,
               xh, wv, wt, xt, gainv, shiftv, bins, hist, gown, dmat, dgrad, dpre, acc, small,
               wpart, wland, wsum, sland, ssum,
               load_s, hx_s, hx_r, hc_s, hc_r, wt_s, wt_r, d_s, d_r, ch_s, ch_r, pa_s, pa_r, pb_s, pb_r,
               z_s, z_r, zs_s, zs_r, y_s, y_r, ys_s, ys_r, ag_s, ag_r):
    sections, nz, ny, micro, rows, channels = sizes
    bulk = nz * ny
    ext = rows + 2 * HALO
    wide = 2 * HALO
    half = rows // 2
    unit = half + 2 * HALO
    blk = 3 * channels // nz
    cols = channels // PARTS
    own_count = micro // 2
    units = 2 * own_count
    s = lax.axis_index("section")
    b = lax.axis_index("bulk")
    c = lax.rem(s, 2)
    z = lax.rem(b, nz)
    y = b // nz
    peer = s + 1 - 2 * c
    left = lax.rem(b + bulk - 1, bulk)
    right = lax.rem(b + 1, bulk)
    first_chip = s >= sections - 2
    later_chip = s < sections - 2
    passes_on = s >= 2
    mine = own_count * c
    theirs = own_count * (1 - c)

    def z_peer(k):
        return y * nz + lax.rem(z + k, nz)

    def y_peer(k):
        return lax.rem(y + k, ny) * nz + z

    barrier = pltpu.get_barrier_semaphore()

    def greet(sec, blk_id):
        pl.semaphore_signal(barrier, inc=1, device_id=(sec, blk_id), device_id_type=MESH)

    greet(s, left)
    greet(s, right)
    greet(peer, b)

    @pl.when(passes_on)
    def _():
        greet(s - 2, b)

    @pl.when(later_chip)
    def _():
        greet(s + 2, b)

    for k in range(1, ny):
        greet(s, y_peer(k))
    for k in range(1, nz):
        greet(s, z_peer(k))

    def local(src, dst, k):
        return pltpu.make_async_copy(src, dst, load_s.at[k])

    loads = [
        local(w_ref.at[0], wv, 0),
        local(x_ref.at[0], xh.at[:, pl.ds(wide, rows)], 1),
        local(gain_ref, gainv, 2),
        local(shift_ref, shiftv, 3),
    ]
    for one in loads:
        one.start()
    cot_loads = [
        local(cot_ref.at[pl.ds(mine, own_count), pl.ds(0, unit - HALO)], hist.at[0, :, 0, pl.ds(HALO, unit - HALO)], 4),
        local(cot_ref.at[pl.ds(mine, own_count), pl.ds(rows - unit + HALO, unit - HALO)], hist.at[0, :, 1, pl.ds(0, unit - HALO)], 5),
    ]

    @pl.when(first_chip)
    def _():
        for one in cot_loads:
            one.start()

    for m in range(micro):
        bins[m] = bins_ref[m]
    loads[0].wait()
    for k in range(3):
        wt[c, k] = wv[k].astype(F32).T.astype(BF16)

    chain_peers = jnp.where(passes_on, 1, 0) + jnp.where(later_chip, 1, 0)
    pl.semaphore_wait(barrier, 3 + (nz - 1) + (ny - 1) + chain_peers)

    def copy(src, dst, send, recv, to):
        return pltpu.make_async_remote_copy(src_ref=src, dst_ref=dst, send_sem=send, recv_sem=recv, device_id=to, device_id_type=MESH)

    x_right = copy(x_ref.at[0, :, pl.ds(rows - wide, wide)], xh.at[:, pl.ds(0, wide)], hx_s.at[0], hx_r.at[0], (s, right))
    x_left = copy(x_ref.at[0, :, pl.ds(0, wide)], xh.at[:, pl.ds(wide + rows, wide)], hx_s.at[1], hx_r.at[1], (s, left))
    c_right = copy(cot_ref.at[pl.ds(mine, own_count), pl.ds(rows - HALO, HALO)], hist.at[0, :, 0, pl.ds(0, HALO)], hc_s.at[0], hc_r.at[0], (s, right))
    c_left = copy(cot_ref.at[pl.ds(mine, own_count), pl.ds(0, HALO)], hist.at[0, :, 1, pl.ds(unit - HALO, HALO)], hc_s.at[1], hc_r.at[1], (s, left))
    w_peer = copy(wt.at[c], wt.at[c], wt_s.at[0], wt_r.at[0], (peer, b))
    x_right.start()
    x_left.start()

    @pl.when(first_chip)
    def _():
        c_right.start()
        c_left.start()

    w_peer.start()
    for one in loads[1:]:
        one.wait()
    x_right.wait_recv()
    x_left.wait_recv()

    def d_copy(j):
        m = theirs + j
        return copy(dmat.at[c, m], dmat.at[c, m], d_s.at[j], d_r.at[j], (peer, b))

    def forward(j, carry):
        m = lax.rem(theirs + j, micro)
        xs = xh[m]
        pre = rolled(dot(xs, wv[0]), 1) + dot(xs, wv[1]) + rolled(dot(xs, wv[2]), -1)
        pre = pre[HALO:HALO + ext]
        k = bins[m]
        gain = gainv[k]
        filmed = pre * gain + shiftv[k]
        sig = jax.nn.sigmoid(filmed)
        d = sig * (1.0 + filmed * (1.0 - sig))
        dmat[c, m] = d * gain

        @pl.when(j < own_count)
        def _():
            d_copy(j).start()

        d = d[HALO:HALO + rows]
        dgrad[m] = d
        dpre[m] = d * pre[HALO:HALO + rows]
        return carry

    lax.fori_loop(0, micro, forward, 0)

    def turn(m, carry):
        xs = xh[m].astype(F32)
        for j, sh in enumerate((1, 0, -1)):
            part = rolled(xs, sh) if sh else xs
            xt[m, j * channels:(j + 1) * channels] = part[wide:wide + rows].T.astype(BF16)
        return carry

    acc[...] = jnp.zeros_like(acc)

    def weight_step(m):
        g = gown[m].astype(F32)
        gp = (g * dmat[c, m, HALO:HALO + rows]).astype(BF16)
        acc[...] += dot(xt[m], gp)
        small[pl.ds(m, 1)] = jnp.sum(g * dpre[m], 0, keepdims=True)
        small[pl.ds(micro + m, 1)] = jnp.sum(g * dgrad[m], 0, keepdims=True)

    @pl.when(later_chip)
    def _():
        lax.fori_loop(0, micro, turn, 0)

    @pl.when(first_chip)
    def _():
        for one in cot_loads:
            one.wait()
        c_right.wait_recv()
        c_left.wait_recv()

    w_peer.wait_recv()

    def split(u):
        i = u // 2
        return i, u - 2 * i

    def chain_copy(u):
        i, h = split(u)
        return copy(hist.at[2, i, h], hist.at[0, i, h], ch_s.at[u], ch_r.at[u], (s - 2, b))

    def spot_of(u):
        i, h = split(u)
        return mine + i, pl.ds(pl.multiple_of(h * half, half), half)

    def grad_copy(u):
        i, h = split(u)
        m, at = spot_of(u)
        return copy(hist.at[c, i, h, pl.ds(HALO, half)], gown.at[m, at], pa_s.at[u], pa_r.at[u], (peer, b))

    def out_copy(u):
        i, h = split(u)
        m, at = spot_of(u)
        return copy(hist.at[c + 1, i, h, pl.ds(HALO, half)], din_ref.at[m, at], pb_s.at[u], pb_r.at[u], (peer, b))

    def back(g, sec, m, at):
        gp = (g * dmat[sec, m, at]).astype(BF16)
        out = g + dot(gp, wt[sec, 1])
        out = out + rolled(dot(gp, wt[sec, 0]), -1)
        out = out + rolled(dot(gp, wt[sec, 2]), 1)
        return out.astype(BF16)

    def chain(u, carry):
        i, h = split(u)
        m, at = spot_of(u)
        span = pl.ds(pl.multiple_of(h * half, half), unit)

        @pl.when(h == 0)
        def _():
            d_copy(i).wait_recv()

        @pl.when(later_chip)
        def _():
            chain_copy(u).wait_recv()

        upper = back(hist[0, i, h].astype(F32), 1, m, span)
        hist[1, i, h] = upper
        lower = back(upper.astype(F32), 0, m, span)
        hist[2, i, h] = lower

        @pl.when(passes_on)
        def _():
            chain_copy(u).start()

        grad_copy(u).start()
        out_copy(u).start()
        gown[m, at] = hist[1 - c, i, h, HALO:HALO + half]
        din_ref[m, at] = hist[2 - c, i, h, HALO:HALO + half]

        @pl.when(later_chip & (h == 1))
        def _():
            weight_step(m)

        @pl.when(later_chip & (h == 0) & (i > 0))
        def _():
            grad_copy(u - 2).wait_recv()
            grad_copy(u - 1).wait_recv()
            weight_step(theirs + i - 1)

        return carry

    lax.fori_loop(0, units, chain, 0)

    @pl.when(first_chip)
    def _():
        lax.fori_loop(0, micro, turn, 0)
        for i in range(own_count):
            weight_step(mine + i)
        for i in range(own_count - 1):
            grad_copy(2 * i).wait_recv()
            grad_copy(2 * i + 1).wait_recv()
            weight_step(theirs + i)

    grad_copy(units - 2).wait_recv()
    grad_copy(units - 1).wait_recv()
    weight_step(theirs + own_count - 1)

    def scatter(q, k):
        to = lax.rem(z + k, nz)
        return copy(wpart.at[q, to], wland.at[q, k], z_s.at[q, k], z_r.at[q, k], (s, y * nz + to))

    def small_z(k):
        return copy(small, sland.at[k], zs_s.at[k], zs_r.at[k], (s, z_peer(k)))

    def across(q, k):
        return copy(wsum.at[q, y], wsum.at[q, y], y_s.at[q, k], y_r.at[q, k], (s, y_peer(k)))

    def small_y(k):
        return copy(ssum.at[y], ssum.at[y], ys_s.at[k], ys_r.at[k], (s, y_peer(k)))

    def gather(q, k):
        return copy(wgather.at[q, z], wgather.at[q, z], ag_s.at[q, k], ag_r.at[q, k], (s, z_peer(k)))

    for q in range(PARTS):
        for j in range(nz):
            wpart[q, j] = acc[j * blk:(j + 1) * blk, q * cols:(q + 1) * cols].astype(BF16)
        for k in range(1, nz):
            scatter(q, k).start()
    for k in range(1, nz):
        small_z(k).start()

    for q in range(PARTS):
        total = wpart[q, z].astype(F32)
        for k in range(1, nz):
            scatter(q, k).wait_recv()
            total = total + wland[q, k].astype(F32)
        wsum[q, y] = total.astype(BF16)
        for k in range(1, ny):
            across(q, k).start()

    sland[0] = small[...]
    for k in range(1, nz):
        small_z(k).wait_recv()
    tiny = sland[z]
    for j in range(1, nz):
        tiny = tiny + sland[lax.rem(z + nz - j, nz)]
    ssum[y] = tiny
    for k in range(1, ny):
        small_y(k).start()

    for q in range(PARTS):
        for k in range(1, ny):
            across(q, k).wait_recv()
        total = wsum[q, 0].astype(F32)
        for j in range(1, ny):
            total = total + wsum[q, j].astype(F32)
        wgather[q, z] = total.astype(BF16)
        for k in range(1, nz):
            gather(q, k).start()

    for k in range(1, ny):
        small_y(k).wait_recv()
    tiny = ssum[0]
    for j in range(1, ny):
        tiny = tiny + ssum[j]
    tiny_ref[...] = tiny

    x_right.wait_send()
    x_left.wait_send()
    w_peer.wait_send()

    @pl.when(first_chip)
    def _():
        c_right.wait_send()
        c_left.wait_send()

    for j in range(own_count):
        d_copy(j).wait_send()
    for u in range(units):
        grad_copy(u).wait_send()
        out_copy(u).wait()

    @pl.when(passes_on)
    def _():
        for u in range(units):
            chain_copy(u).wait_send()

    for k in range(1, nz):
        small_z(k).wait_send()
    for k in range(1, ny):
        small_y(k).wait_send()
    for q in range(PARTS):
        for k in range(1, nz):
            scatter(q, k).wait_send()
        for k in range(1, ny):
            across(q, k).wait_send()
        for k in range(1, nz):
            gather(q, k).wait()


def finish_body(din_ref, wgather, tiny_ref, bins_ref, din_out, dw_out, gain_out, shift_out, wide_w, gains, shifts, sems):
    parts, nz, blk, cols = wgather.shape
    micro = tiny_ref.shape[0] // 2
    channels = cols * parts
    copies = [pltpu.make_async_copy(din_ref, din_out.at[0], sems.at[0])]
    copies[0].start()
    for j in range(nz):
        for q in range(parts):
            wide_w[j * blk:(j + 1) * blk, q * cols:(q + 1) * cols] = wgather[q, j].astype(F32)
    copies.append(pltpu.make_async_copy(wide_w, dw_out.at[0], sems.at[1]))
    copies[1].start()
    count = gains.shape[0]
    spot = lax.broadcasted_iota(jnp.int32, (count, 1, channels), 0)
    out_gain = jnp.zeros((count, 1, channels), F32)
    out_shift = jnp.zeros((count, 1, channels), F32)
    for m in range(micro):
        hit = spot == bins_ref[m]
        out_gain = out_gain + jnp.where(hit, tiny_ref[m:m + 1][None], 0.0)
        out_shift = out_shift + jnp.where(hit, tiny_ref[micro + m:micro + m + 1][None], 0.0)
    gains[...] = out_gain
    shifts[...] = out_shift
    copies.append(pltpu.make_async_copy(gains, gain_out, sems.at[2]))
    copies.append(pltpu.make_async_copy(shifts, shift_out, sems.at[3]))
    copies[2].start()
    copies[3].start()
    for one in copies:
        one.wait()


def shards(sections, bulk, activations, weights, film_gain, film_shift, doa_bins, cotangent):
    micro, rows, channels = activations.shape[1:]
    bins_count = film_gain.shape[1]
    nz = 8 if bulk == 32 else 2
    ny = bulk // nz
    ext = rows + 2 * HALO
    blk = 3 * channels // nz
    cols = channels // PARTS
    own = micro // 2
    unit = rows // 2 + 2 * HALO
    sizes = (sections, nz, ny, micro, rows, channels)
    dma = pltpu.SemaphoreType.DMA
    vmem = pl.BlockSpec(memory_space=pltpu.VMEM)
    hbm = pl.BlockSpec(memory_space=pltpu.HBM)
    smem = pl.BlockSpec(memory_space=pltpu.SMEM)
    scratch = pltpu.VMEM
    gain_rows = jnp.transpose(film_gain, (1, 0, 2))
    shift_rows = jnp.transpose(film_shift, (1, 0, 2))
    d_in, w_sum, tiny = pl.pallas_call(
        functools.partial(chain_body, sizes),
        out_shape=(
            jax.ShapeDtypeStruct((micro, rows, channels), BF16),
            jax.ShapeDtypeStruct((PARTS, nz, blk, cols), BF16),
            jax.ShapeDtypeStruct((2 * micro, channels), F32),
        ),
        in_specs=[hbm, hbm, hbm, hbm, smem, hbm],
        out_specs=(vmem, vmem, vmem),
        scratch_shapes=[
            scratch((micro, ext + 2 * HALO, channels), BF16),
            scratch((3, channels, channels), BF16),
            scratch((2, 3, channels, channels), BF16),
            scratch((micro, 3 * channels, rows), BF16),
            scratch((bins_count, 1, channels), F32),
            scratch((bins_count, 1, channels), F32),
            pltpu.SMEM((micro,), jnp.int32),
            scratch((3, own, 2, unit, channels), BF16),
            scratch((micro, rows, channels), BF16),
            scratch((2, micro, ext, channels), F32),
            scratch((micro, rows, channels), F32),
            scratch((micro, rows, channels), F32),
            scratch((3 * channels, channels), F32),
            scratch((2 * micro, channels), F32),
            scratch((PARTS, nz, blk, cols), BF16),
            scratch((PARTS, nz, blk, cols), BF16),
            scratch((PARTS, ny, blk, cols), BF16),
            scratch((nz, 2 * micro, channels), F32),
            scratch((ny, 2 * micro, channels), F32),
            dma((6,)), dma((2,)), dma((2,)), dma((2,)), dma((2,)), dma((1,)), dma((1,)),
            dma((own,)), dma((own,)), dma((2 * own,)), dma((2 * own,)),
            dma((2 * own,)), dma((2 * own,)), dma((2 * own,)), dma((2 * own,)),
            dma((PARTS, nz)), dma((PARTS, nz)), dma((nz,)), dma((nz,)),
            dma((PARTS, ny)), dma((PARTS, ny)), dma((ny,)), dma((ny,)),
            dma((PARTS, nz)), dma((PARTS, nz)),
        ],
        compiler_params=pltpu.CompilerParams(
            collective_id=0, has_side_effects=True, vmem_limit_bytes=48 * 1024 * 1024
        ),
    )(activations, weights, gain_rows, shift_rows, doa_bins, cotangent)
    d_in, d_w, d_gain, d_shift = pl.pallas_call(
        finish_body,
        out_shape=(
            jax.ShapeDtypeStruct((1, micro, rows, channels), BF16),
            jax.ShapeDtypeStruct((1, 3 * channels, channels), F32),
            jax.ShapeDtypeStruct((bins_count, 1, channels), F32),
            jax.ShapeDtypeStruct((bins_count, 1, channels), F32),
        ),
        in_specs=[vmem, vmem, vmem, smem],
        out_specs=(hbm, hbm, hbm, hbm),
        scratch_shapes=[
            scratch((3 * channels, channels), F32),
            scratch((bins_count, 1, channels), F32),
            scratch((bins_count, 1, channels), F32),
            dma((4,)),
        ],
        compiler_params=pltpu.CompilerParams(vmem_limit_bytes=16 * 1024 * 1024),
    )(d_in, w_sum, tiny, doa_bins)
    return (
        d_in,
        d_w.reshape(1, 3, channels, channels),
        jnp.transpose(d_gain, (1, 0, 2)),
        jnp.transpose(d_shift, (1, 0, 2)),
    )


def solution(mesh):
    return jax.shard_map(
        functools.partial(shards, mesh.shape["section"], mesh.shape["bulk"]),
        mesh=mesh,
        in_specs=(
            P("section", None, "bulk", None),
            P("section", None, None, None),
            P("section", None, None),
            P("section", None, None),
            P(),
            P(None, "bulk", None),
        ),
        out_specs=(
            P("section", None, "bulk", None),
            P("section", None, None, None),
            P("section", None, None),
            P("section", None, None),
        ),
        check_vma=False,
    )
```

```python
import functools

import jax
import jax.numpy as jnp
from jax import lax
from jax.experimental import pallas as pl
from jax.experimental.pallas import tpu as pltpu
from jax.sharding import PartitionSpec as P

MESH = pl.DeviceIdType.MESH
F32 = jnp.float32
BF16 = jnp.bfloat16
HALO = 16
ROW_PARTS = 2
COL_PARTS = 2
PARTS = ROW_PARTS * COL_PARTS
SPLIT = 4


def rolled(value, shift):
    return pltpu.roll(value, shift % value.shape[0], 0)


def dot(left, right):
    return jnp.dot(left, right, preferred_element_type=F32)


def chain_body(sizes, x_ref, w_ref, gain_ref, shift_ref, bins_ref, cot_ref,
               din_ref, dw_ref, gain_out, shift_out,
               xh, wv, wt, xt, gainv, shiftv, bins, hist, gown, dmat, dgrad, dpre, acc, small,
               wpart, wland, wsum, wgather, wide_w, gains, shifts, sland, ssum,
               load_s, own_s, store_s, hx_s, hx_r, hc_s, hc_r, wt_s, wt_r, d_s, d_r, ch_s, ch_r, pa_s, pa_r, pb_s, pb_r,
               z_s, z_r, zs_s, zs_r, y_s, y_r, ys_s, ys_r, ag_s, ag_r):
    sections, nz, ny, micro, rows, channels = sizes
    bulk = nz * ny
    ext = rows + 2 * HALO
    wide = 2 * HALO
    half = rows // SPLIT
    unit = half + 2 * HALO
    blk = 3 * channels // nz
    sub = blk // ROW_PARTS
    cols = channels // COL_PARTS
    own_count = micro // 2
    units = SPLIT * own_count
    z_order = sorted(range(1, nz), key=lambda k: -min(k, nz - k))
    y_order = sorted(range(1, ny), key=lambda k: -min(k, ny - k))
    s = lax.axis_index("section")
    b = lax.axis_index("bulk")
    c = lax.rem(s, 2)
    z = lax.rem(b, nz)
    y = b // nz
    peer = s + 1 - 2 * c
    left = lax.rem(b + bulk - 1, bulk)
    right = lax.rem(b + 1, bulk)
    first_chip = s >= sections - 2
    later_chip = s < sections - 2
    passes_on = s >= 2
    mine = own_count * c
    theirs = own_count * (1 - c)

    def z_peer(k):
        return y * nz + lax.rem(z + k, nz)

    def y_peer(k):
        return lax.rem(y + k, ny) * nz + z

    barrier = pltpu.get_barrier_semaphore()

    def greet(sec, blk_id):
        pl.semaphore_signal(barrier, inc=1, device_id=(sec, blk_id), device_id_type=MESH)

    greet(s, left)
    greet(s, right)
    greet(peer, b)

    @pl.when(passes_on)
    def _():
        greet(s - 2, b)

    @pl.when(later_chip)
    def _():
        greet(s + 2, b)

    for k in range(1, ny):
        greet(s, y_peer(k))
    for k in range(1, nz):
        greet(s, z_peer(k))

    def local(src, dst, k):
        return pltpu.make_async_copy(src, dst, load_s.at[k])

    loads = [
        local(w_ref.at[0], wv, 0),
        local(x_ref.at[0], xh.at[:, pl.ds(wide, rows)], 1),
        local(gain_ref, gainv, 2),
        local(shift_ref, shiftv, 3),
    ]
    for one in loads:
        one.start()
    cot_loads = []
    for h in range(SPLIT):
        start = max(0, half * h - HALO)
        count = min(rows, half * h + half + HALO) - start
        cot_loads.append(local(
            cot_ref.at[pl.ds(mine, own_count), pl.ds(start, count)],
            hist.at[0, :, h, pl.ds(start - half * h + HALO, count)], 4 + h))

    @pl.when(first_chip)
    def _():
        for one in cot_loads:
            one.start()

    for m in range(micro):
        bins[m] = bins_ref[m]
    loads[0].wait()
    for k in range(3):
        wt[c, k] = wv[k].astype(F32).T.astype(BF16)

    chain_peers = jnp.where(passes_on, 1, 0) + jnp.where(later_chip, 1, 0)
    pl.semaphore_wait(barrier, 3 + (nz - 1) + (ny - 1) + chain_peers)

    def copy(src, dst, send, recv, to):
        return pltpu.make_async_remote_copy(src_ref=src, dst_ref=dst, send_sem=send, recv_sem=recv, device_id=to, device_id_type=MESH)

    x_right = copy(x_ref.at[0, :, pl.ds(rows - wide, wide)], xh.at[:, pl.ds(0, wide)], hx_s.at[0], hx_r.at[0], (s, right))
    x_left = copy(x_ref.at[0, :, pl.ds(0, wide)], xh.at[:, pl.ds(wide + rows, wide)], hx_s.at[1], hx_r.at[1], (s, left))
    c_right = copy(cot_ref.at[pl.ds(mine, own_count), pl.ds(rows - HALO, HALO)], hist.at[0, :, 0, pl.ds(0, HALO)], hc_s.at[0], hc_r.at[0], (s, right))
    c_left = copy(cot_ref.at[pl.ds(mine, own_count), pl.ds(0, HALO)], hist.at[0, :, SPLIT - 1, pl.ds(unit - HALO, HALO)], hc_s.at[1], hc_r.at[1], (s, left))
    w_peer = copy(wt.at[c], wt.at[c], wt_s.at[0], wt_r.at[0], (peer, b))
    x_right.start()
    x_left.start()

    @pl.when(first_chip)
    def _():
        c_right.start()
        c_left.start()

    w_peer.start()
    for one in loads[1:]:
        one.wait()

    def taps(xs):
        return rolled(dot(xs, wv[0]), 1) + dot(xs, wv[1]) + rolled(dot(xs, wv[2]), -1)

    def film(pre, k):
        gain = gainv[k]
        filmed = pre * gain + shiftv[k]
        sig = jax.nn.sigmoid(filmed)
        d = sig * (1.0 + filmed * (1.0 - sig))
        return d, d * gain

    def inner(m, carry):
        pre = taps(xh[m, wide:wide + rows])
        d, full = film(pre, bins[m])
        dmat[c, m, HALO:HALO + rows] = full
        dgrad[m] = d
        dpre[m] = d * pre
        return carry

    lax.fori_loop(0, micro, inner, 0)
    x_right.wait_recv()
    x_left.wait_recv()

    def d_copy(j):
        m = theirs + j
        return copy(dmat.at[c, m], dmat.at[c, m], d_s.at[j], d_r.at[j], (peer, b))

    def forward(j, carry):
        m = lax.rem(theirs + j, micro)
        ends = jnp.concatenate([xh[m, 0:2 * wide], xh[m, rows:rows + 2 * wide]], axis=0)
        pre = taps(ends)
        d, full = film(pre, bins[m])
        low = slice(HALO, HALO + wide)
        high = slice(2 * wide + HALO, 3 * wide + HALO)
        dmat[c, m, 0:wide] = full[low]
        dmat[c, m, rows:rows + wide] = full[high]

        @pl.when(j < own_count)
        def _():
            d_copy(j).start()

        both = d * pre
        dgrad[m, 0:HALO] = d[wide:wide + HALO]
        dpre[m, 0:HALO] = both[wide:wide + HALO]
        dgrad[m, rows - HALO:rows] = d[high][0:HALO]
        dpre[m, rows - HALO:rows] = both[high][0:HALO]
        return carry

    lax.fori_loop(0, micro, forward, 0)

    def turn(m, carry):
        xs = xh[m].astype(F32)
        for j, sh in enumerate((1, 0, -1)):
            part = rolled(xs, sh) if sh else xs
            xt[m, j * channels:(j + 1) * channels] = part[wide:wide + rows].T.astype(BF16)
        return carry

    acc[...] = jnp.zeros_like(acc)

    def weight_step(m):
        g = gown[m].astype(F32)
        gp = (g * dmat[c, m, HALO:HALO + rows]).astype(BF16)
        acc[...] += dot(xt[m], gp)
        small[pl.ds(m, 1)] = jnp.sum(g * dpre[m], 0, keepdims=True)
        small[pl.ds(micro + m, 1)] = jnp.sum(g * dgrad[m], 0, keepdims=True)

    @pl.when(later_chip)
    def _():
        lax.fori_loop(0, micro, turn, 0)

    @pl.when(first_chip)
    def _():
        for one in cot_loads:
            one.wait()
        c_right.wait_recv()
        c_left.wait_recv()

    w_peer.wait_recv()

    def split(u):
        i = u // SPLIT
        return i, u - SPLIT * i

    def chain_copy(u):
        i, h = split(u)
        return copy(hist.at[2, i, h], hist.at[0, i, h], ch_s.at[u], ch_r.at[u], (s - 2, b))

    def spot_of(u):
        i, h = split(u)
        return mine + i, pl.ds(pl.multiple_of(h * half, half), half)

    def grad_copy(u):
        i, h = split(u)
        m, at = spot_of(u)
        return copy(hist.at[c, i, h, pl.ds(HALO, half)], gown.at[m, at], pa_s.at[u], pa_r.at[u], (peer, b))

    def out_copy(u):
        i, h = split(u)
        m, at = spot_of(u)
        return copy(hist.at[c + 1, i, h, pl.ds(HALO, half)], din_ref.at[m, at], pb_s.at[u], pb_r.at[u], (peer, b))

    def own_copy(u):
        i, h = split(u)
        m, at = spot_of(u)
        return pltpu.make_async_copy(hist.at[2 - c, i, h, pl.ds(HALO, half)], din_ref.at[m, at], own_s.at[u])

    def back(g, sec, m, at):
        gp = (g * dmat[sec, m, at]).astype(BF16)
        out = g + dot(gp, wt[sec, 1])
        out = out + rolled(dot(gp, wt[sec, 0]), -1)
        out = out + rolled(dot(gp, wt[sec, 2]), 1)
        return out.astype(BF16)

    def chain(u, carry):
        i, h = split(u)
        m, at = spot_of(u)
        span = pl.ds(pl.multiple_of(h * half, half), unit)

        @pl.when(h == 0)
        def _():
            d_copy(i).wait_recv()

        @pl.when(later_chip)
        def _():
            chain_copy(u).wait_recv()

        upper = back(hist[0, i, h].astype(F32), 1, m, span)
        hist[1, i, h] = upper
        lower = back(upper.astype(F32), 0, m, span)
        hist[2, i, h] = lower

        @pl.when(passes_on)
        def _():
            chain_copy(u).start()

        grad_copy(u).start()
        out_copy(u).start()
        own_copy(u).start()
        gown[m, at] = hist[1 - c, i, h, HALO:HALO + half]

        @pl.when(later_chip & (h == SPLIT - 1))
        def _():
            weight_step(m)

        @pl.when(later_chip & (h == 0) & (i > 0))
        def _():
            for k in range(SPLIT):
                grad_copy(u - SPLIT + k).wait_recv()
            weight_step(theirs + i - 1)

        return carry

    lax.fori_loop(0, units, chain, 0)

    @pl.when(first_chip)
    def _():
        lax.fori_loop(0, micro, turn, 0)
        for i in range(own_count):
            weight_step(mine + i)
        for i in range(own_count - 1):
            for k in range(SPLIT):
                grad_copy(SPLIT * i + k).wait_recv()
            weight_step(theirs + i)

    for k in range(SPLIT):
        grad_copy(units - SPLIT + k).wait_recv()
    weight_step(theirs + own_count - 1)

    def scatter(q, k):
        to = lax.rem(z + k, nz)
        return copy(wpart.at[q, to], wland.at[q, k], z_s.at[q, k], z_r.at[q, k], (s, y * nz + to))

    def small_z(k):
        return copy(small, sland.at[k], zs_s.at[k], zs_r.at[k], (s, z_peer(k)))

    def across(q, k):
        return copy(wsum.at[q, y], wsum.at[q, y], y_s.at[q, k], y_r.at[q, k], (s, y_peer(k)))

    def small_y(k):
        return copy(ssum.at[y], ssum.at[y], ys_s.at[k], ys_r.at[k], (s, y_peer(k)))

    def gather(q, k):
        return copy(wgather.at[q, z], wgather.at[q, z], ag_s.at[q, k], ag_r.at[q, k], (s, z_peer(k)))

    def area(q, j):
        top, side = j * blk + (q // COL_PARTS) * sub, (q % COL_PARTS) * cols
        return slice(top, top + sub), slice(side, side + cols)

    for q in range(PARTS):
        for j in range(nz):
            at_rows, at_cols = area(q, j)
            wpart[q, j] = acc[at_rows, at_cols].astype(BF16)
        for k in z_order:
            scatter(q, k).start()
    for k in z_order:
        small_z(k).start()

    for q in range(PARTS):
        total = wpart[q, z].astype(F32)
        for k in z_order:
            scatter(q, k).wait_recv()
            total = total + wland[q, k].astype(F32)
        wsum[q, y] = total.astype(BF16)
        for k in y_order:
            across(q, k).start()

    sland[0] = small[...]
    for k in range(1, nz):
        small_z(k).wait_recv()
    tiny = sland[z]
    for j in range(1, nz):
        tiny = tiny + sland[lax.rem(z + nz - j, nz)]
    ssum[y] = tiny
    for k in y_order:
        small_y(k).start()

    for q in range(PARTS):
        for k in range(1, ny):
            across(q, k).wait_recv()
        total = wsum[q, 0].astype(F32)
        for j in range(1, ny):
            total = total + wsum[q, j].astype(F32)
        wgather[q, z] = total.astype(BF16)
        for k in z_order:
            gather(q, k).start()

    for k in range(1, ny):
        small_y(k).wait_recv()
    tiny = ssum[0]
    for j in range(1, ny):
        tiny = tiny + ssum[j]
    count = gains.shape[0]
    spot = lax.broadcasted_iota(jnp.int32, (count, 1, channels), 0)
    sum_gain = jnp.zeros((count, 1, channels), F32)
    sum_shift = jnp.zeros((count, 1, channels), F32)
    for m in range(micro):
        hit = spot == bins[m]
        sum_gain = sum_gain + jnp.where(hit, tiny[m:m + 1][None], 0.0)
        sum_shift = sum_shift + jnp.where(hit, tiny[micro + m:micro + m + 1][None], 0.0)
    gains[...] = sum_gain
    shifts[...] = sum_shift
    stores = [
        pltpu.make_async_copy(gains, gain_out, store_s.at[0]),
        pltpu.make_async_copy(shifts, shift_out, store_s.at[1]),
    ]
    for one in stores:
        one.start()

    x_right.wait_send()
    x_left.wait_send()
    w_peer.wait_send()

    @pl.when(first_chip)
    def _():
        c_right.wait_send()
        c_left.wait_send()

    for j in range(own_count):
        d_copy(j).wait_send()
    for u in range(units):
        grad_copy(u).wait_send()
        out_copy(u).wait()
        own_copy(u).wait()

    @pl.when(passes_on)
    def _():
        for u in range(units):
            chain_copy(u).wait_send()

    for k in range(1, nz):
        small_z(k).wait_send()
    for k in range(1, ny):
        small_y(k).wait_send()
    for q in range(PARTS):
        for k in range(1, nz):
            gather(q, k).wait()
        for j in range(nz):
            at_rows, at_cols = area(q, j)
            wide_w[at_rows, at_cols] = wgather[q, j].astype(F32)
    stores.append(pltpu.make_async_copy(wide_w, dw_ref, store_s.at[2]))
    stores[2].start()
    for one in stores:
        one.wait()
    for q in range(PARTS):
        for k in range(1, nz):
            scatter(q, k).wait_send()
        for k in range(1, ny):
            across(q, k).wait_send()


def finish_body(din_ref, dw_ref, gain_ref, shift_ref, din_out, dw_out, gain_out, shift_out, din, dw, gains, shifts, load_s, store_s):
    micro = din_ref.shape[0]
    tap = dw_ref.shape[0] // 3
    trips = [(dw_ref.at[pl.ds(k * tap, tap)], dw.at[k], dw_out.at[0, k]) for k in range(3)]
    trips += [(din_ref.at[m], din.at[m], din_out.at[0, m]) for m in range(micro)]
    trips += [(gain_ref, gains, gain_out), (shift_ref, shifts, shift_out)]
    loads = [pltpu.make_async_copy(src, mid, load_s.at[k]) for k, (src, mid, _) in enumerate(trips)]
    stores = [pltpu.make_async_copy(mid, dst, store_s.at[k]) for k, (_, mid, dst) in enumerate(trips)]
    for one in loads:
        one.start()
    for one, two in zip(loads, stores):
        one.wait()
        two.start()
    for two in stores:
        two.wait()


def shards(sections, bulk, activations, weights, film_gain, film_shift, doa_bins, cotangent):
    micro, rows, channels = activations.shape[1:]
    bins_count = film_gain.shape[1]
    nz = 8 if bulk == 32 else 2
    ny = bulk // nz
    ext = rows + 2 * HALO
    blk = 3 * channels // nz
    sub = blk // ROW_PARTS
    cols = channels // COL_PARTS
    own = micro // 2
    units = SPLIT * own
    unit = rows // SPLIT + 2 * HALO
    sizes = (sections, nz, ny, micro, rows, channels)
    dma = pltpu.SemaphoreType.DMA
    hbm = pl.BlockSpec(memory_space=pltpu.HBM)
    smem = pl.BlockSpec(memory_space=pltpu.SMEM)
    scratch = pltpu.VMEM
    gain_rows = jnp.transpose(film_gain, (1, 0, 2))
    shift_rows = jnp.transpose(film_shift, (1, 0, 2))
    held = pl.pallas_call(
        functools.partial(chain_body, sizes),
        out_shape=(
            jax.ShapeDtypeStruct((micro, rows, channels), BF16),
            jax.ShapeDtypeStruct((3 * channels, channels), F32),
            jax.ShapeDtypeStruct((bins_count, 1, channels), F32),
            jax.ShapeDtypeStruct((bins_count, 1, channels), F32),
        ),
        in_specs=[hbm, hbm, hbm, hbm, smem, hbm],
        out_specs=(hbm, hbm, hbm, hbm),
        scratch_shapes=[
            scratch((micro, ext + 2 * HALO, channels), BF16),
            scratch((3, channels, channels), BF16),
            scratch((2, 3, channels, channels), BF16),
            scratch((micro, 3 * channels, rows), BF16),
            scratch((bins_count, 1, channels), F32),
            scratch((bins_count, 1, channels), F32),
            pltpu.SMEM((micro,), jnp.int32),
            scratch((3, own, SPLIT, unit, channels), BF16),
            scratch((micro, rows, channels), BF16),
            scratch((2, micro, ext, channels), F32),
            scratch((micro, rows, channels), F32),
            scratch((micro, rows, channels), F32),
            scratch((3 * channels, channels), F32),
            scratch((2 * micro, channels), F32),
            scratch((PARTS, nz, sub, cols), BF16),
            scratch((PARTS, nz, sub, cols), BF16),
            scratch((PARTS, ny, sub, cols), BF16),
            scratch((PARTS, nz, sub, cols), BF16),
            scratch((3 * channels, channels), F32),
            scratch((bins_count, 1, channels), F32),
            scratch((bins_count, 1, channels), F32),
            scratch((nz, 2 * micro, channels), F32),
            scratch((ny, 2 * micro, channels), F32),
            dma((4 + SPLIT,)), dma((units,)), dma((3,)),
            dma((2,)), dma((2,)), dma((2,)), dma((2,)), dma((1,)), dma((1,)),
            dma((own,)), dma((own,)), dma((units,)), dma((units,)),
            dma((units,)), dma((units,)), dma((units,)), dma((units,)),
            dma((PARTS, nz)), dma((PARTS, nz)), dma((nz,)), dma((nz,)),
            dma((PARTS, ny)), dma((PARTS, ny)), dma((ny,)), dma((ny,)),
            dma((PARTS, nz)), dma((PARTS, nz)),
        ],
        compiler_params=pltpu.CompilerParams(
            collective_id=0, has_side_effects=True, vmem_limit_bytes=60 * 1024 * 1024
        ),
    )(activations, weights, gain_rows, shift_rows, doa_bins, cotangent)
    d_in, d_w, d_gain, d_shift = pl.pallas_call(
        finish_body,
        out_shape=(
            jax.ShapeDtypeStruct((1, micro, rows, channels), BF16),
            jax.ShapeDtypeStruct((1, 3, channels, channels), F32),
            jax.ShapeDtypeStruct((bins_count, 1, channels), F32),
            jax.ShapeDtypeStruct((bins_count, 1, channels), F32),
        ),
        in_specs=[hbm, hbm, hbm, hbm],
        out_specs=(hbm, hbm, hbm, hbm),
        scratch_shapes=[
            scratch((micro, rows, channels), BF16),
            scratch((3, channels, channels), F32),
            scratch((bins_count, 1, channels), F32),
            scratch((bins_count, 1, channels), F32),
            dma((3 + micro + 2,)),
            dma((3 + micro + 2,)),
        ],
        compiler_params=pltpu.CompilerParams(vmem_limit_bytes=60 * 1024 * 1024),
    )(*held)
    return (
        d_in,
        d_w,
        jnp.transpose(d_gain, (1, 0, 2)),
        jnp.transpose(d_shift, (1, 0, 2)),
    )


def solution(mesh):
    return jax.shard_map(
        functools.partial(shards, mesh.shape["section"], mesh.shape["bulk"]),
        mesh=mesh,
        in_specs=(
            P("section", None, "bulk", None),
            P("section", None, None, None),
            P("section", None, None),
            P("section", None, None),
            P(),
            P(None, "bulk", None),
        ),
        out_specs=(
            P("section", None, "bulk", None),
            P("section", None, None, None),
            P("section", None, None),
            P("section", None, None),
        ),
        check_vma=False,
    )
```

```python
import functools

import jax
import jax.numpy as jnp
from jax import lax
from jax.experimental import pallas as pl
from jax.experimental.pallas import tpu as pltpu
from jax.sharding import PartitionSpec as P

MESH = pl.DeviceIdType.MESH
F32 = jnp.float32
BF16 = jnp.bfloat16
HALO = 16
ROW_PARTS = 2
COL_PARTS = 2
PARTS = ROW_PARTS * COL_PARTS
SPLIT = 4


def rolled(value, shift):
    return pltpu.roll(value, shift % value.shape[0], 0)


def dot(left, right):
    return jnp.dot(left, right, preferred_element_type=F32)


def chain_body(sizes, x_ref, w_ref, gain_ref, shift_ref, bins_ref, cot_ref,
               din_ref, dw_ref, gain_out, shift_out,
               xh, wv, wt, xt, gainv, shiftv, bins, hist, gown, dmat, dgrad, dpre, acc, small,
               wpart, wland, wsum, wgather, wide_w, gains, shifts, sland, ssum,
               load_s, own_s, store_s, hx_s, hx_r, hc_s, hc_r, wt_s, wt_r, d_s, d_r, ch_s, ch_r, pa_s, pa_r, pb_s, pb_r,
               z_s, z_r, zs_s, zs_r, y_s, y_r, ys_s, ys_r, ag_s, ag_r):
    sections, nz, ny, micro, rows, channels = sizes
    bulk = nz * ny
    ext = rows + 2 * HALO
    wide = 2 * HALO
    half = rows // SPLIT
    unit = half + 2 * HALO
    blk = 3 * channels // nz
    sub = blk // ROW_PARTS
    cols = channels // COL_PARTS
    own_count = micro // 2
    units = SPLIT * own_count
    middles = 2 * own_count
    z_order = sorted(range(1, nz), key=lambda k: -min(k, nz - k))
    y_order = sorted(range(1, ny), key=lambda k: -min(k, ny - k))
    s = lax.axis_index("section")
    b = lax.axis_index("bulk")
    c = lax.rem(s, 2)
    z = lax.rem(b, nz)
    y = b // nz
    peer = s + 1 - 2 * c
    left = lax.rem(b + bulk - 1, bulk)
    right = lax.rem(b + 1, bulk)
    first_chip = s >= sections - 2
    later_chip = s < sections - 2
    passes_on = s >= 2
    mine = own_count * c
    theirs = own_count * (1 - c)

    def z_peer(k):
        return y * nz + lax.rem(z + k, nz)

    def y_peer(k):
        return lax.rem(y + k, ny) * nz + z

    barrier = pltpu.get_barrier_semaphore()

    def greet(sec, blk_id):
        pl.semaphore_signal(barrier, inc=1, device_id=(sec, blk_id), device_id_type=MESH)

    greet(s, left)
    greet(s, right)
    greet(peer, b)

    @pl.when(passes_on)
    def _():
        greet(s - 2, b)

    @pl.when(later_chip)
    def _():
        greet(s + 2, b)

    for k in range(1, ny):
        greet(s, y_peer(k))
    for k in range(1, nz):
        greet(s, z_peer(k))

    def local(src, dst, k):
        return pltpu.make_async_copy(src, dst, load_s.at[k])

    loads = [
        local(w_ref.at[0], wv, 0),
        local(x_ref.at[0], xh.at[:, pl.ds(wide, rows)], 1),
        local(gain_ref, gainv, 2),
        local(shift_ref, shiftv, 3),
    ]
    for one in loads:
        one.start()
    cot_loads = []
    for h in range(SPLIT):
        start = max(0, half * h - HALO)
        count = min(rows, half * h + half + HALO) - start
        cot_loads.append(local(
            cot_ref.at[pl.ds(mine, own_count), pl.ds(start, count)],
            hist.at[0, :, h, pl.ds(start - half * h + HALO, count)], 4 + h))

    @pl.when(first_chip)
    def _():
        for one in cot_loads:
            one.start()

    for m in range(micro):
        bins[m] = bins_ref[m]
    loads[0].wait()
    for k in range(3):
        wt[c, k] = wv[k].astype(F32).T.astype(BF16)

    for one in loads[1:]:
        one.wait()

    def taps(xs):
        return rolled(dot(xs, wv[0]), 1) + dot(xs, wv[1]) + rolled(dot(xs, wv[2]), -1)

    def film(pre, k):
        gain = gainv[k]
        filmed = pre * gain + shiftv[k]
        sig = jax.nn.sigmoid(filmed)
        d = sig * (1.0 + filmed * (1.0 - sig))
        return d, d * gain

    def inner(j, carry):
        m = lax.rem(theirs + j, micro)
        pre = taps(xh[m, wide:wide + rows])
        d, full = film(pre, bins[m])
        dmat[c, m, HALO:HALO + rows] = full
        dgrad[m] = d
        dpre[m] = d * pre
        return carry

    lax.fori_loop(0, own_count, inner, 0)

    chain_peers = jnp.where(passes_on, 1, 0) + jnp.where(later_chip, 1, 0)
    pl.semaphore_wait(barrier, 3 + (nz - 1) + (ny - 1) + chain_peers)

    def copy(src, dst, send, recv, to):
        return pltpu.make_async_remote_copy(src_ref=src, dst_ref=dst, send_sem=send, recv_sem=recv, device_id=to, device_id_type=MESH)

    x_right = copy(x_ref.at[0, :, pl.ds(rows - wide, wide)], xh.at[:, pl.ds(0, wide)], hx_s.at[0], hx_r.at[0], (s, right))
    x_left = copy(x_ref.at[0, :, pl.ds(0, wide)], xh.at[:, pl.ds(wide + rows, wide)], hx_s.at[1], hx_r.at[1], (s, left))
    c_right = copy(cot_ref.at[pl.ds(mine, own_count), pl.ds(rows - HALO, HALO)], hist.at[0, :, 0, pl.ds(0, HALO)], hc_s.at[0], hc_r.at[0], (s, right))
    c_left = copy(cot_ref.at[pl.ds(mine, own_count), pl.ds(0, HALO)], hist.at[0, :, SPLIT - 1, pl.ds(unit - HALO, HALO)], hc_s.at[1], hc_r.at[1], (s, left))
    w_peer = copy(wt.at[c], wt.at[c], wt_s.at[0], wt_r.at[0], (peer, b))
    d_spans = (pl.ds(wide, rows - wide), pl.ds(0, wide), pl.ds(rows, wide))

    def d_copy(j, part):
        at = dmat.at[c, theirs + j, d_spans[part]]
        return copy(at, at, d_s.at[j, part], d_r.at[j, part], (peer, b))

    x_right.start()
    x_left.start()
    for j in range(own_count):
        d_copy(j, 0).start()
    w_peer.start()

    @pl.when(first_chip)
    def _():
        c_right.start()
        c_left.start()

    lax.fori_loop(own_count, micro, inner, 0)

    def outer(j, carry):
        m = lax.rem(theirs + j, micro)
        ends = jnp.concatenate([xh[m, 0:2 * wide], xh[m, rows:rows + 2 * wide]], axis=0)
        pre = taps(ends)
        d, full = film(pre, bins[m])
        low = slice(HALO, HALO + wide)
        high = slice(2 * wide + HALO, 3 * wide + HALO)
        dmat[c, m, 0:wide] = full[low]
        dmat[c, m, rows:rows + wide] = full[high]

        @pl.when(j < own_count)
        def _():
            d_copy(j, 1).start()
            d_copy(j, 2).start()

        both = d * pre
        dgrad[m, 0:HALO] = d[wide:wide + HALO]
        dpre[m, 0:HALO] = both[wide:wide + HALO]
        dgrad[m, rows - HALO:rows] = d[high][0:HALO]
        dpre[m, rows - HALO:rows] = both[high][0:HALO]
        return carry

    def ends_forward():
        x_right.wait_recv()
        x_left.wait_recv()
        lax.fori_loop(0, micro, outer, 0)

    def turn(m, carry):
        xs = xh[m].astype(F32)
        for j, sh in enumerate((1, 0, -1)):
            part = rolled(xs, sh) if sh else xs
            xt[m, j * channels:(j + 1) * channels] = part[wide:wide + rows].T.astype(BF16)
        return carry

    acc[...] = jnp.zeros_like(acc)

    def weight_step(m):
        g = gown[m].astype(F32)
        gp = (g * dmat[c, m, HALO:HALO + rows]).astype(BF16)
        acc[...] += dot(xt[m], gp)
        small[pl.ds(m, 1)] = jnp.sum(g * dpre[m], 0, keepdims=True)
        small[pl.ds(micro + m, 1)] = jnp.sum(g * dgrad[m], 0, keepdims=True)

    @pl.when(later_chip)
    def _():
        ends_forward()
        lax.fori_loop(0, micro, turn, 0)

    @pl.when(first_chip)
    def _():
        for one in cot_loads:
            one.wait()

    w_peer.wait_recv()

    def split(u):
        late = u // middles
        side = u % 2
        i = (u % middles) // 2
        return i, (1 - late) * (1 + side) + late * (SPLIT - 1) * side

    def units_of(i):
        return [2 * i, 2 * i + 1, middles + 2 * i, middles + 2 * i + 1]

    def chain_copy(u):
        i, h = split(u)
        return copy(hist.at[2, i, h], hist.at[0, i, h], ch_s.at[u], ch_r.at[u], (s - 2, b))

    def spot_of(u):
        i, h = split(u)
        return mine + i, pl.ds(pl.multiple_of(h * half, half), half)

    def grad_copy(u):
        i, h = split(u)
        m, at = spot_of(u)
        return copy(hist.at[c, i, h, pl.ds(HALO, half)], gown.at[m, at], pa_s.at[u], pa_r.at[u], (peer, b))

    def out_copy(u):
        i, h = split(u)
        m, at = spot_of(u)
        return copy(hist.at[c + 1, i, h, pl.ds(HALO, half)], din_ref.at[m, at], pb_s.at[u], pb_r.at[u], (peer, b))

    def own_copy(u):
        i, h = split(u)
        m, at = spot_of(u)
        return pltpu.make_async_copy(hist.at[2 - c, i, h, pl.ds(HALO, half)], din_ref.at[m, at], own_s.at[u])

    def back(g, sec, m, at):
        gp = (g * dmat[sec, m, at]).astype(BF16)
        out = g + dot(gp, wt[sec, 1])
        out = out + rolled(dot(gp, wt[sec, 0]), -1)
        out = out + rolled(dot(gp, wt[sec, 2]), 1)
        return out.astype(BF16)

    def chain(u, carry):
        i, h = split(u)
        m, at = spot_of(u)
        span = pl.ds(pl.multiple_of(h * half, half), unit)

        @pl.when(first_chip & (u == middles - 1))
        def _():
            ends_forward()

        @pl.when(h == 1)
        def _():
            d_copy(i, 0).wait_recv()

        @pl.when(h == 0)
        def _():
            d_copy(i, 1).wait_recv()
            d_copy(i, 2).wait_recv()

        @pl.when(first_chip & (u == middles))
        def _():
            c_right.wait_recv()
            c_left.wait_recv()

        @pl.when(later_chip)
        def _():
            chain_copy(u).wait_recv()

        upper = back(hist[0, i, h].astype(F32), 1, m, span)
        hist[1, i, h] = upper
        lower = back(upper.astype(F32), 0, m, span)
        hist[2, i, h] = lower

        @pl.when(passes_on)
        def _():
            chain_copy(u).start()

        grad_copy(u).start()
        out_copy(u).start()
        own_copy(u).start()
        gown[m, at] = hist[1 - c, i, h, HALO:HALO + half]

        @pl.when(later_chip & (h == SPLIT - 1))
        def _():
            weight_step(m)

        @pl.when(later_chip & (h == 0) & (i > 0))
        def _():
            for k in units_of(i - 1):
                grad_copy(k).wait_recv()
            weight_step(theirs + i - 1)

        return carry

    lax.fori_loop(0, units, chain, 0)

    @pl.when(first_chip)
    def _():
        lax.fori_loop(0, micro, turn, 0)
        for i in range(own_count):
            weight_step(mine + i)
        for i in range(own_count - 1):
            for k in units_of(i):
                grad_copy(k).wait_recv()
            weight_step(theirs + i)

    for k in units_of(own_count - 1):
        grad_copy(k).wait_recv()
    weight_step(theirs + own_count - 1)

    def scatter(q, k):
        to = lax.rem(z + k, nz)
        return copy(wpart.at[q, to], wland.at[q, k], z_s.at[q, k], z_r.at[q, k], (s, y * nz + to))

    def small_z(k):
        return copy(small, sland.at[k], zs_s.at[k], zs_r.at[k], (s, z_peer(k)))

    def across(q, k):
        return copy(wsum.at[q, y], wsum.at[q, y], y_s.at[q, k], y_r.at[q, k], (s, y_peer(k)))

    def small_y(k):
        return copy(ssum.at[y], ssum.at[y], ys_s.at[k], ys_r.at[k], (s, y_peer(k)))

    def gather(q, k):
        return copy(wgather.at[q, z], wgather.at[q, z], ag_s.at[q, k], ag_r.at[q, k], (s, z_peer(k)))

    def area(q, j):
        top, side = j * blk + (q // COL_PARTS) * sub, (q % COL_PARTS) * cols
        return slice(top, top + sub), slice(side, side + cols)

    for q in range(PARTS):
        for j in range(nz):
            at_rows, at_cols = area(q, j)
            wpart[q, j] = acc[at_rows, at_cols].astype(BF16)
        for k in z_order:
            scatter(q, k).start()
    for k in z_order:
        small_z(k).start()

    for q in range(PARTS):
        total = wpart[q, z].astype(F32)
        for k in z_order:
            scatter(q, k).wait_recv()
            total = total + wland[q, k].astype(F32)
        wsum[q, y] = total.astype(BF16)
        for k in y_order:
            across(q, k).start()

    sland[0] = small[...]
    for k in range(1, nz):
        small_z(k).wait_recv()
    tiny = sland[z]
    for j in range(1, nz):
        tiny = tiny + sland[lax.rem(z + nz - j, nz)]
    ssum[y] = tiny
    for k in y_order:
        small_y(k).start()

    for q in range(PARTS):
        for k in range(1, ny):
            across(q, k).wait_recv()
        total = wsum[q, 0].astype(F32)
        for j in range(1, ny):
            total = total + wsum[q, j].astype(F32)
        wgather[q, z] = total.astype(BF16)
        for k in z_order:
            gather(q, k).start()

    for k in range(1, ny):
        small_y(k).wait_recv()
    tiny = ssum[0]
    for j in range(1, ny):
        tiny = tiny + ssum[j]
    count = gains.shape[0]
    spot = lax.broadcasted_iota(jnp.int32, (count, 1, channels), 0)
    sum_gain = jnp.zeros((count, 1, channels), F32)
    sum_shift = jnp.zeros((count, 1, channels), F32)
    for m in range(micro):
        hit = spot == bins[m]
        sum_gain = sum_gain + jnp.where(hit, tiny[m:m + 1][None], 0.0)
        sum_shift = sum_shift + jnp.where(hit, tiny[micro + m:micro + m + 1][None], 0.0)
    gains[...] = sum_gain
    shifts[...] = sum_shift
    stores = [
        pltpu.make_async_copy(gains, gain_out, store_s.at[0]),
        pltpu.make_async_copy(shifts, shift_out, store_s.at[1]),
    ]
    for one in stores:
        one.start()

    x_right.wait_send()
    x_left.wait_send()
    w_peer.wait_send()

    @pl.when(first_chip)
    def _():
        c_right.wait_send()
        c_left.wait_send()

    for j in range(own_count):
        for part in range(3):
            d_copy(j, part).wait_send()
    for u in range(units):
        grad_copy(u).wait_send()
        out_copy(u).wait()
        own_copy(u).wait()

    @pl.when(passes_on)
    def _():
        for u in range(units):
            chain_copy(u).wait_send()

    for k in range(1, nz):
        small_z(k).wait_send()
    for k in range(1, ny):
        small_y(k).wait_send()
    for q in range(PARTS):
        for k in range(1, nz):
            gather(q, k).wait()
        for j in range(nz):
            at_rows, at_cols = area(q, j)
            wide_w[at_rows, at_cols] = wgather[q, j].astype(F32)
    stores.append(pltpu.make_async_copy(wide_w, dw_ref, store_s.at[2]))
    stores[2].start()
    for one in stores:
        one.wait()
    for q in range(PARTS):
        for k in range(1, nz):
            scatter(q, k).wait_send()
        for k in range(1, ny):
            across(q, k).wait_send()


def finish_body(din_ref, dw_ref, gain_ref, shift_ref, din_out, dw_out, gain_out, shift_out, din, dw, gains, shifts, load_s, store_s):
    micro = din_ref.shape[0]
    tap = dw_ref.shape[0] // 3
    trips = [(dw_ref.at[pl.ds(k * tap, tap)], dw.at[k], dw_out.at[0, k]) for k in range(3)]
    trips += [(din_ref.at[m], din.at[m], din_out.at[0, m]) for m in range(micro)]
    trips += [(gain_ref, gains, gain_out), (shift_ref, shifts, shift_out)]
    loads = [pltpu.make_async_copy(src, mid, load_s.at[k]) for k, (src, mid, _) in enumerate(trips)]
    stores = [pltpu.make_async_copy(mid, dst, store_s.at[k]) for k, (_, mid, dst) in enumerate(trips)]
    for one in loads:
        one.start()
    for one, two in zip(loads, stores):
        one.wait()
        two.start()
    for two in stores:
        two.wait()


def shards(sections, bulk, activations, weights, film_gain, film_shift, doa_bins, cotangent):
    micro, rows, channels = activations.shape[1:]
    bins_count = film_gain.shape[1]
    nz = 8 if bulk == 32 else 2
    ny = bulk // nz
    ext = rows + 2 * HALO
    blk = 3 * channels // nz
    sub = blk // ROW_PARTS
    cols = channels // COL_PARTS
    own = micro // 2
    units = SPLIT * own
    unit = rows // SPLIT + 2 * HALO
    sizes = (sections, nz, ny, micro, rows, channels)
    dma = pltpu.SemaphoreType.DMA
    hbm = pl.BlockSpec(memory_space=pltpu.HBM)
    smem = pl.BlockSpec(memory_space=pltpu.SMEM)
    scratch = pltpu.VMEM
    gain_rows = jnp.transpose(film_gain, (1, 0, 2))
    shift_rows = jnp.transpose(film_shift, (1, 0, 2))
    held = pl.pallas_call(
        functools.partial(chain_body, sizes),
        out_shape=(
            jax.ShapeDtypeStruct((micro, rows, channels), BF16),
            jax.ShapeDtypeStruct((3 * channels, channels), F32),
            jax.ShapeDtypeStruct((bins_count, 1, channels), F32),
            jax.ShapeDtypeStruct((bins_count, 1, channels), F32),
        ),
        in_specs=[hbm, hbm, hbm, hbm, smem, hbm],
        out_specs=(hbm, hbm, hbm, hbm),
        scratch_shapes=[
            scratch((micro, ext + 2 * HALO, channels), BF16),
            scratch((3, channels, channels), BF16),
            scratch((2, 3, channels, channels), BF16),
            scratch((micro, 3 * channels, rows), BF16),
            scratch((bins_count, 1, channels), F32),
            scratch((bins_count, 1, channels), F32),
            pltpu.SMEM((micro,), jnp.int32),
            scratch((3, own, SPLIT, unit, channels), BF16),
            scratch((micro, rows, channels), BF16),
            scratch((2, micro, ext, channels), F32),
            scratch((micro, rows, channels), F32),
            scratch((micro, rows, channels), F32),
            scratch((3 * channels, channels), F32),
            scratch((2 * micro, channels), F32),
            scratch((PARTS, nz, sub, cols), BF16),
            scratch((PARTS, nz, sub, cols), BF16),
            scratch((PARTS, ny, sub, cols), BF16),
            scratch((PARTS, nz, sub, cols), BF16),
            scratch((3 * channels, channels), F32),
            scratch((bins_count, 1, channels), F32),
            scratch((bins_count, 1, channels), F32),
            scratch((nz, 2 * micro, channels), F32),
            scratch((ny, 2 * micro, channels), F32),
            dma((4 + SPLIT,)), dma((units,)), dma((3,)),
            dma((2,)), dma((2,)), dma((2,)), dma((2,)), dma((1,)), dma((1,)),
            dma((own, 3)), dma((own, 3)), dma((units,)), dma((units,)),
            dma((units,)), dma((units,)), dma((units,)), dma((units,)),
            dma((PARTS, nz)), dma((PARTS, nz)), dma((nz,)), dma((nz,)),
            dma((PARTS, ny)), dma((PARTS, ny)), dma((ny,)), dma((ny,)),
            dma((PARTS, nz)), dma((PARTS, nz)),
        ],
        compiler_params=pltpu.CompilerParams(
            collective_id=0, has_side_effects=True, vmem_limit_bytes=60 * 1024 * 1024
        ),
    )(activations, weights, gain_rows, shift_rows, doa_bins, cotangent)
    d_in, d_w, d_gain, d_shift = pl.pallas_call(
        finish_body,
        out_shape=(
            jax.ShapeDtypeStruct((1, micro, rows, channels), BF16),
            jax.ShapeDtypeStruct((1, 3, channels, channels), F32),
            jax.ShapeDtypeStruct((bins_count, 1, channels), F32),
            jax.ShapeDtypeStruct((bins_count, 1, channels), F32),
        ),
        in_specs=[hbm, hbm, hbm, hbm],
        out_specs=(hbm, hbm, hbm, hbm),
        scratch_shapes=[
            scratch((micro, rows, channels), BF16),
            scratch((3, channels, channels), F32),
            scratch((bins_count, 1, channels), F32),
            scratch((bins_count, 1, channels), F32),
            dma((3 + micro + 2,)),
            dma((3 + micro + 2,)),
        ],
        compiler_params=pltpu.CompilerParams(vmem_limit_bytes=60 * 1024 * 1024),
    )(*held)
    return (
        d_in,
        d_w,
        jnp.transpose(d_gain, (1, 0, 2)),
        jnp.transpose(d_shift, (1, 0, 2)),
    )


def solution(mesh):
    return jax.shard_map(
        functools.partial(shards, mesh.shape["section"], mesh.shape["bulk"]),
        mesh=mesh,
        in_specs=(
            P("section", None, "bulk", None),
            P("section", None, None, None),
            P("section", None, None),
            P("section", None, None),
            P(),
            P(None, "bulk", None),
        ),
        out_specs=(
            P("section", None, "bulk", None),
            P("section", None, None, None),
            P("section", None, None),
            P("section", None, None),
        ),
        check_vma=False,
    )
```

```python
import functools

import jax
import jax.numpy as jnp
from jax import lax
from jax.experimental import pallas as pl
from jax.experimental.pallas import tpu as pltpu
from jax.sharding import PartitionSpec as P

MESH = pl.DeviceIdType.MESH
F32 = jnp.float32
BF16 = jnp.bfloat16
HALO = 16
ROW_PARTS = 2
COL_PARTS = 2
PARTS = ROW_PARTS * COL_PARTS
SPLIT = 4


def rolled(value, shift):
    return pltpu.roll(value, shift % value.shape[0], 0)


def dot(left, right):
    return jnp.dot(left, right, preferred_element_type=F32)


def chain_body(sizes, x_ref, w_ref, gain_ref, shift_ref, bins_ref, cot_ref,
               din_ref, dw_ref, gain_out, shift_out,
               xh, wv, wt, xt, gainv, shiftv, bins, hist, gown, dmat, dgrad, dpre, acc, small,
               wpart, wland, wsum, wgather, wide_w, gains, shifts, sland, ssum,
               load_s, own_s, store_s, hx_s, hx_r, hc_s, hc_r, wt_s, wt_r, d_s, d_r, ch_s, ch_r, pa_s, pa_r, pb_s, pb_r,
               z_s, z_r, zs_s, zs_r, y_s, y_r, ys_s, ys_r, ag_s, ag_r):
    sections, nz, ny, micro, rows, channels = sizes
    bulk = nz * ny
    ext = rows + 2 * HALO
    wide = 2 * HALO
    half = rows // SPLIT
    unit = half + 2 * HALO
    blk = 3 * channels // nz
    sub = blk // ROW_PARTS
    cols = channels // COL_PARTS
    own_count = micro // 2
    units = SPLIT * own_count
    middles = 2 * own_count
    z_order = sorted(range(1, nz), key=lambda k: -min(k, nz - k))
    y_order = sorted(range(1, ny), key=lambda k: -min(k, ny - k))
    s = lax.axis_index("section")
    b = lax.axis_index("bulk")
    c = lax.rem(s, 2)
    z = lax.rem(b, nz)
    y = b // nz
    peer = s + 1 - 2 * c
    left = lax.rem(b + bulk - 1, bulk)
    right = lax.rem(b + 1, bulk)
    first_chip = s >= sections - 2
    later_chip = s < sections - 2
    passes_on = s >= 2
    mine = own_count * c
    theirs = own_count * (1 - c)

    def z_peer(k):
        return y * nz + lax.rem(z + k, nz)

    def y_peer(k):
        return lax.rem(y + k, ny) * nz + z

    barrier = pltpu.get_barrier_semaphore()

    def greet(sec, blk_id):
        pl.semaphore_signal(barrier, inc=1, device_id=(sec, blk_id), device_id_type=MESH)

    greet(s, left)
    greet(s, right)
    greet(peer, b)

    @pl.when(passes_on)
    def _():
        greet(s - 2, b)

    @pl.when(later_chip)
    def _():
        greet(s + 2, b)

    for k in range(1, ny):
        greet(s, y_peer(k))
    for k in range(1, nz):
        greet(s, z_peer(k))

    def local(src, dst, k):
        return pltpu.make_async_copy(src, dst, load_s.at[k])

    loads = [
        local(w_ref.at[0], wv, 0),
        local(x_ref.at[0], xh.at[:, pl.ds(wide, rows)], 1),
        local(gain_ref, gainv, 2),
        local(shift_ref, shiftv, 3),
    ]
    for one in loads:
        one.start()
    cot_loads = []
    for h in range(SPLIT):
        start = max(0, half * h - HALO)
        count = min(rows, half * h + half + HALO) - start
        cot_loads.append(local(
            cot_ref.at[pl.ds(mine, own_count), pl.ds(start, count)],
            hist.at[0, :, h, pl.ds(start - half * h + HALO, count)], 4 + h))

    @pl.when(first_chip)
    def _():
        for one in cot_loads:
            one.start()

    for m in range(micro):
        bins[m] = bins_ref[m]
    loads[0].wait()
    for k in range(3):
        wt[c, k] = wv[k].astype(F32).T.astype(BF16)

    for one in loads[1:]:
        one.wait()

    def taps(xs):
        return rolled(dot(xs, wv[0]), 1) + dot(xs, wv[1]) + rolled(dot(xs, wv[2]), -1)

    def film(pre, k):
        gain = gainv[k]
        filmed = pre * gain + shiftv[k]
        sig = jax.nn.sigmoid(filmed)
        d = sig * (1.0 + filmed * (1.0 - sig))
        return d, d * gain

    def inner(j, carry):
        m = lax.rem(theirs + j, micro)
        pre = taps(xh[m, wide:wide + rows])
        d, full = film(pre, bins[m])
        dmat[c, m, HALO:HALO + rows] = full
        dgrad[m] = d
        dpre[m] = d * pre
        return carry

    lax.fori_loop(0, own_count, inner, 0)

    chain_peers = jnp.where(passes_on, 1, 0) + jnp.where(later_chip, 1, 0)
    pl.semaphore_wait(barrier, 3 + (nz - 1) + (ny - 1) + chain_peers)

    def copy(src, dst, send, recv, to):
        return pltpu.make_async_remote_copy(src_ref=src, dst_ref=dst, send_sem=send, recv_sem=recv, device_id=to, device_id_type=MESH)

    x_right = copy(x_ref.at[0, :, pl.ds(rows - wide, wide)], xh.at[:, pl.ds(0, wide)], hx_s.at[0], hx_r.at[0], (s, right))
    x_left = copy(x_ref.at[0, :, pl.ds(0, wide)], xh.at[:, pl.ds(wide + rows, wide)], hx_s.at[1], hx_r.at[1], (s, left))
    c_right = copy(cot_ref.at[pl.ds(mine, own_count), pl.ds(rows - HALO, HALO)], hist.at[0, :, 0, pl.ds(0, HALO)], hc_s.at[0], hc_r.at[0], (s, right))
    c_left = copy(cot_ref.at[pl.ds(mine, own_count), pl.ds(0, HALO)], hist.at[0, :, SPLIT - 1, pl.ds(unit - HALO, HALO)], hc_s.at[1], hc_r.at[1], (s, left))
    w_peer = copy(wt.at[c], wt.at[c], wt_s.at[0], wt_r.at[0], (peer, b))
    d_spans = (pl.ds(wide, rows - wide), pl.ds(0, wide), pl.ds(rows, wide))

    def d_copy(j, part):
        at = dmat.at[c, theirs + j, d_spans[part]]
        return copy(at, at, d_s.at[j, part], d_r.at[j, part], (peer, b))

    x_right.start()
    x_left.start()
    d_copy(0, 0).start()
    w_peer.start()
    for j in range(1, own_count):
        d_copy(j, 0).start()

    @pl.when(first_chip)
    def _():
        c_right.start()
        c_left.start()

    lax.fori_loop(own_count, micro, inner, 0)

    def outer(j, carry):
        m = lax.rem(theirs + j, micro)
        ends = jnp.concatenate([xh[m, 0:2 * wide], xh[m, rows:rows + 2 * wide]], axis=0)
        pre = taps(ends)
        d, full = film(pre, bins[m])
        low = slice(HALO, HALO + wide)
        high = slice(2 * wide + HALO, 3 * wide + HALO)
        dmat[c, m, 0:wide] = full[low]
        dmat[c, m, rows:rows + wide] = full[high]

        @pl.when(j < own_count)
        def _():
            d_copy(j, 1).start()
            d_copy(j, 2).start()

        both = d * pre
        dgrad[m, 0:HALO] = d[wide:wide + HALO]
        dpre[m, 0:HALO] = both[wide:wide + HALO]
        dgrad[m, rows - HALO:rows] = d[high][0:HALO]
        dpre[m, rows - HALO:rows] = both[high][0:HALO]
        return carry

    def ends_forward():
        x_right.wait_recv()
        x_left.wait_recv()
        lax.fori_loop(0, micro, outer, 0)

    def turn(m, carry):
        xs = xh[m].astype(F32)
        for j, sh in enumerate((1, 0, -1)):
            part = rolled(xs, sh) if sh else xs
            xt[lax.rem(m, own_count), m // own_count, j * channels:(j + 1) * channels] = part[wide:wide + rows].T.astype(BF16)
        return carry

    acc[...] = jnp.zeros_like(acc)

    def pair_term(i):
        both = []
        for k in range(2):
            m = own_count * k + i
            g = gown[m].astype(F32)
            both.append((g * dmat[c, m, HALO:HALO + rows]).astype(BF16))
            small[pl.ds(m, 1)] = jnp.sum(g * dpre[m], 0, keepdims=True)
            small[pl.ds(micro + m, 1)] = jnp.sum(g * dgrad[m], 0, keepdims=True)
        left_side = jnp.concatenate([xt[i, 0], xt[i, 1]], axis=1)
        return dot(left_side, jnp.concatenate(both, axis=0))

    def weight_pair(i):
        for k in units_of(i):
            grad_copy(k).wait_recv()
        acc[...] += pair_term(i)

    @pl.when(later_chip)
    def _():
        ends_forward()
        lax.fori_loop(0, micro, turn, 0)

    @pl.when(first_chip)
    def _():
        for one in cot_loads:
            one.wait()

    w_peer.wait_recv()

    def split(u):
        late = u // middles
        side = u % 2
        i = (u % middles) // 2
        return i, (1 - late) * (1 + side) + late * (SPLIT - 1) * side

    def units_of(i):
        return [2 * i, 2 * i + 1, middles + 2 * i, middles + 2 * i + 1]

    def chain_copy(u, whole):
        i, h = split(u)
        at = pl.ds(0, unit) if whole else pl.ds(pl.multiple_of(h // 2 * HALO, HALO), unit - HALO)
        return copy(hist.at[2, i, h, at], hist.at[0, i, h, at], ch_s.at[u], ch_r.at[u], (s - 2, b))

    def side_halo(i, h):
        upper_half = h // 2
        to = pl.multiple_of((1 - upper_half) * (unit - HALO), HALO)
        source = upper_half * (h - 1) + 1 - upper_half
        start = pl.multiple_of(HALO + upper_half * (half - HALO), HALO)
        hist[0, i, h, pl.ds(to, HALO)] = hist[0, i, source, pl.ds(start, HALO)]

    def spot_of(u):
        i, h = split(u)
        return mine + i, pl.ds(pl.multiple_of(h * half, half), half)

    def grad_copy(u):
        i, h = split(u)
        m, at = spot_of(u)
        return copy(hist.at[c, i, h, pl.ds(HALO, half)], gown.at[m, at], pa_s.at[u], pa_r.at[u], (peer, b))

    def out_copy(u):
        i, h = split(u)
        m, at = spot_of(u)
        return copy(hist.at[c + 1, i, h, pl.ds(HALO, half)], din_ref.at[m, at], pb_s.at[u], pb_r.at[u], (peer, b))

    def own_copy(u):
        i, h = split(u)
        m, at = spot_of(u)
        return pltpu.make_async_copy(hist.at[2 - c, i, h, pl.ds(HALO, half)], din_ref.at[m, at], own_s.at[u])

    def back(g, sec, m, at):
        gp = (g * dmat[sec, m, at]).astype(BF16)
        out = g + dot(gp, wt[sec, 1])
        out = out + rolled(dot(gp, wt[sec, 0]), -1)
        out = out + rolled(dot(gp, wt[sec, 2]), 1)
        return out.astype(BF16)

    def chain(u, carry):
        i, h = split(u)
        m, at = spot_of(u)
        span = pl.ds(pl.multiple_of(h * half, half), unit)

        @pl.when(first_chip & (u == middles - 1))
        def _():
            ends_forward()

        @pl.when(h == 1)
        def _():
            d_copy(i, 0).wait_recv()

        @pl.when(h == 0)
        def _():
            d_copy(i, 1).wait_recv()
            d_copy(i, 2).wait_recv()

        @pl.when(first_chip & (u == middles))
        def _():
            c_right.wait_recv()
            c_left.wait_recv()

        @pl.when(later_chip & (h == 1))
        def _():
            chain_copy(u, True).wait_recv()

        @pl.when(later_chip & (h != 1))
        def _():
            chain_copy(u, False).wait_recv()
            side_halo(i, h)

        upper = back(hist[0, i, h].astype(F32), 1, m, span)
        hist[1, i, h] = upper
        grad_copy(u).start()
        lower = back(upper.astype(F32), 0, m, span)
        hist[2, i, h] = lower

        @pl.when(passes_on & (h == 1))
        def _():
            chain_copy(u, True).start()

        @pl.when(passes_on & (h != 1))
        def _():
            chain_copy(u, False).start()

        out_copy(u).start()
        own_copy(u).start()
        gown[m, at] = hist[1 - c, i, h, HALO:HALO + half]

        for k in range(own_count - 1):
            @pl.when(later_chip & (u == middles + 2 * k + 2))
            def _():
                weight_pair(k)

        return carry

    lax.fori_loop(0, units, chain, 0)

    @pl.when(first_chip)
    def _():
        lax.fori_loop(0, micro, turn, 0)
        for i in range(own_count - 1):
            weight_pair(i)

    for k in units_of(own_count - 1):
        grad_copy(k).wait_recv()
    last_term = pair_term(own_count - 1)

    def scatter(q, k):
        to = lax.rem(z + k, nz)
        return copy(wpart.at[q, to], wland.at[q, k], z_s.at[q, k], z_r.at[q, k], (s, y * nz + to))

    def small_z(k):
        return copy(small, sland.at[k], zs_s.at[k], zs_r.at[k], (s, z_peer(k)))

    def across(q, k):
        return copy(wsum.at[q, y], wsum.at[q, y], y_s.at[q, k], y_r.at[q, k], (s, y_peer(k)))

    def small_y(k):
        return copy(ssum.at[y], ssum.at[y], ys_s.at[k], ys_r.at[k], (s, y_peer(k)))

    def gather(q, k):
        return copy(wgather.at[q, z], wgather.at[q, z], ag_s.at[q, k], ag_r.at[q, k], (s, z_peer(k)))

    def area(q, j):
        top, side = j * blk + (q // COL_PARTS) * sub, (q % COL_PARTS) * cols
        return slice(top, top + sub), slice(side, side + cols)

    for q in range(PARTS):
        for j in range(nz):
            at_rows, at_cols = area(q, j)
            wpart[q, j] = (acc[at_rows, at_cols] + last_term[at_rows, at_cols]).astype(BF16)
        for k in z_order:
            scatter(q, k).start()
    for k in z_order:
        small_z(k).start()

    for q in range(PARTS):
        total = wpart[q, z].astype(F32)
        for k in z_order:
            scatter(q, k).wait_recv()
            total = total + wland[q, k].astype(F32)
        wsum[q, y] = total.astype(BF16)
        for k in y_order:
            across(q, k).start()

    sland[0] = small[...]
    for k in range(1, nz):
        small_z(k).wait_recv()
    tiny = sland[z]
    for j in range(1, nz):
        tiny = tiny + sland[lax.rem(z + nz - j, nz)]
    ssum[y] = tiny
    for k in y_order:
        small_y(k).start()

    for q in range(PARTS):
        for k in range(1, ny):
            across(q, k).wait_recv()
        total = wsum[q, 0].astype(F32)
        for j in range(1, ny):
            total = total + wsum[q, j].astype(F32)
        wgather[q, z] = total.astype(BF16)
        for k in z_order:
            gather(q, k).start()

    for k in range(1, ny):
        small_y(k).wait_recv()
    tiny = ssum[0]
    for j in range(1, ny):
        tiny = tiny + ssum[j]
    count = gains.shape[0]
    spot = lax.broadcasted_iota(jnp.int32, (count, 1, channels), 0)
    sum_gain = jnp.zeros((count, 1, channels), F32)
    sum_shift = jnp.zeros((count, 1, channels), F32)
    for m in range(micro):
        hit = spot == bins[m]
        sum_gain = sum_gain + jnp.where(hit, tiny[m:m + 1][None], 0.0)
        sum_shift = sum_shift + jnp.where(hit, tiny[micro + m:micro + m + 1][None], 0.0)
    gains[...] = sum_gain
    shifts[...] = sum_shift
    stores = [
        pltpu.make_async_copy(gains, gain_out, store_s.at[0]),
        pltpu.make_async_copy(shifts, shift_out, store_s.at[1]),
    ]
    for one in stores:
        one.start()

    x_right.wait_send()
    x_left.wait_send()
    w_peer.wait_send()

    @pl.when(first_chip)
    def _():
        c_right.wait_send()
        c_left.wait_send()

    for j in range(own_count):
        for part in range(3):
            d_copy(j, part).wait_send()
    for u in range(units):
        grad_copy(u).wait_send()
        out_copy(u).wait()
        own_copy(u).wait()

    @pl.when(passes_on)
    def _():
        for u in range(units):
            chain_copy(u, split(u)[1] == 1).wait_send()

    for k in range(1, nz):
        small_z(k).wait_send()
    for k in range(1, ny):
        small_y(k).wait_send()
    for q in range(PARTS):
        for k in range(1, nz):
            gather(q, k).wait()
        part, side = q // COL_PARTS, q % COL_PARTS
        for j in range(nz):
            wide_w[j, part, :, side * cols:(side + 1) * cols] = wgather[q, j].astype(F32)
        if side == COL_PARTS - 1:
            stores.append(pltpu.make_async_copy(wide_w.at[:, part], dw_ref.at[:, part], store_s.at[2 + part]))
            stores[-1].start()
    for one in stores:
        one.wait()
    for q in range(PARTS):
        for k in range(1, nz):
            scatter(q, k).wait_send()
        for k in range(1, ny):
            across(q, k).wait_send()


def finish_body(din_ref, dw_ref, gain_ref, shift_ref, din_out, dw_out, gain_out, shift_out, din, dw, gains, shifts, load_s, store_s):
    micro = din_ref.shape[0]
    tap = dw_ref.shape[0] // 3
    trips = [(dw_ref.at[pl.ds(k * tap, tap)], dw.at[k], dw_out.at[0, k]) for k in range(3)]
    trips += [(din_ref.at[m], din.at[m], din_out.at[0, m]) for m in range(micro)]
    trips += [(gain_ref, gains, gain_out), (shift_ref, shifts, shift_out)]
    loads = [pltpu.make_async_copy(src, mid, load_s.at[k]) for k, (src, mid, _) in enumerate(trips)]
    stores = [pltpu.make_async_copy(mid, dst, store_s.at[k]) for k, (_, mid, dst) in enumerate(trips)]
    for one in loads:
        one.start()
    for one, two in zip(loads, stores):
        one.wait()
        two.start()
    for two in stores:
        two.wait()


def shards(sections, bulk, activations, weights, film_gain, film_shift, doa_bins, cotangent):
    micro, rows, channels = activations.shape[1:]
    bins_count = film_gain.shape[1]
    nz = 8 if bulk == 32 else 2
    ny = bulk // nz
    ext = rows + 2 * HALO
    blk = 3 * channels // nz
    sub = blk // ROW_PARTS
    cols = channels // COL_PARTS
    own = micro // 2
    units = SPLIT * own
    unit = rows // SPLIT + 2 * HALO
    sizes = (sections, nz, ny, micro, rows, channels)
    dma = pltpu.SemaphoreType.DMA
    hbm = pl.BlockSpec(memory_space=pltpu.HBM)
    smem = pl.BlockSpec(memory_space=pltpu.SMEM)
    scratch = pltpu.VMEM
    gain_rows = jnp.transpose(film_gain, (1, 0, 2))
    shift_rows = jnp.transpose(film_shift, (1, 0, 2))
    d_in, d_w, d_gain, d_shift = pl.pallas_call(
        functools.partial(chain_body, sizes),
        out_shape=(
            jax.ShapeDtypeStruct((micro, rows, channels), BF16),
            jax.ShapeDtypeStruct((nz, ROW_PARTS, sub, channels), F32),
            jax.ShapeDtypeStruct((bins_count, 1, channels), F32),
            jax.ShapeDtypeStruct((bins_count, 1, channels), F32),
        ),
        in_specs=[hbm, hbm, hbm, hbm, smem, hbm],
        out_specs=(hbm, hbm, hbm, hbm),
        scratch_shapes=[
            scratch((micro, ext + 2 * HALO, channels), BF16),
            scratch((3, channels, channels), BF16),
            scratch((2, 3, channels, channels), BF16),
            scratch((own, 2, 3 * channels, rows), BF16),
            scratch((bins_count, 1, channels), F32),
            scratch((bins_count, 1, channels), F32),
            pltpu.SMEM((micro,), jnp.int32),
            scratch((3, own, SPLIT, unit, channels), BF16),
            scratch((micro, rows, channels), BF16),
            scratch((2, micro, ext, channels), F32),
            scratch((micro, rows, channels), F32),
            scratch((micro, rows, channels), F32),
            scratch((3 * channels, channels), F32),
            scratch((2 * micro, channels), F32),
            scratch((PARTS, nz, sub, cols), BF16),
            scratch((PARTS, nz, sub, cols), BF16),
            scratch((PARTS, ny, sub, cols), BF16),
            scratch((PARTS, nz, sub, cols), BF16),
            scratch((nz, ROW_PARTS, sub, channels), F32),
            scratch((bins_count, 1, channels), F32),
            scratch((bins_count, 1, channels), F32),
            scratch((nz, 2 * micro, channels), F32),
            scratch((ny, 2 * micro, channels), F32),
            dma((4 + SPLIT,)), dma((units,)), dma((2 + ROW_PARTS,)),
            dma((2,)), dma((2,)), dma((2,)), dma((2,)), dma((1,)), dma((1,)),
            dma((own, 3)), dma((own, 3)), dma((units,)), dma((units,)),
            dma((units,)), dma((units,)), dma((units,)), dma((units,)),
            dma((PARTS, nz)), dma((PARTS, nz)), dma((nz,)), dma((nz,)),
            dma((PARTS, ny)), dma((PARTS, ny)), dma((ny,)), dma((ny,)),
            dma((PARTS, nz)), dma((PARTS, nz)),
        ],
        compiler_params=pltpu.CompilerParams(
            collective_id=0, has_side_effects=True, vmem_limit_bytes=60 * 1024 * 1024
        ),
    )(activations, weights, gain_rows, shift_rows, doa_bins, cotangent)
    d_in, d_w, d_gain, d_shift = pl.pallas_call(
        finish_body,
        out_shape=(
            jax.ShapeDtypeStruct((1, micro, rows, channels), BF16),
            jax.ShapeDtypeStruct((1, 3, channels, channels), F32),
            jax.ShapeDtypeStruct((bins_count, 1, channels), F32),
            jax.ShapeDtypeStruct((bins_count, 1, channels), F32),
        ),
        in_specs=[hbm, hbm, hbm, hbm],
        out_specs=(hbm, hbm, hbm, hbm),
        scratch_shapes=[
            scratch((micro, rows, channels), BF16),
            scratch((3, channels, channels), F32),
            scratch((bins_count, 1, channels), F32),
            scratch((bins_count, 1, channels), F32),
            dma((3 + micro + 2,)),
            dma((3 + micro + 2,)),
        ],
        compiler_params=pltpu.CompilerParams(vmem_limit_bytes=60 * 1024 * 1024),
    )(d_in, d_w.reshape(3 * channels, channels), d_gain, d_shift)
    return (
        d_in,
        d_w,
        jnp.transpose(d_gain, (1, 0, 2)),
        jnp.transpose(d_shift, (1, 0, 2)),
    )


def solution(mesh):
    return jax.shard_map(
        functools.partial(shards, mesh.shape["section"], mesh.shape["bulk"]),
        mesh=mesh,
        in_specs=(
            P("section", None, "bulk", None),
            P("section", None, None, None),
            P("section", None, None),
            P("section", None, None),
            P(),
            P(None, "bulk", None),
        ),
        out_specs=(
            P("section", None, "bulk", None),
            P("section", None, None, None),
            P("section", None, None),
            P("section", None, None),
        ),
        check_vma=False,
    )
```

```python
import functools

import jax
import jax.numpy as jnp
from jax import lax
from jax.experimental import pallas as pl
from jax.experimental.pallas import tpu as pltpu
from jax.sharding import PartitionSpec as P

MESH = pl.DeviceIdType.MESH
F32 = jnp.float32
BF16 = jnp.bfloat16
HALO = 16
ROW_PARTS = 2
COL_PARTS = 2
PARTS = ROW_PARTS * COL_PARTS
SPLIT = 4


def rolled(value, shift):
    return pltpu.roll(value, shift % value.shape[0], 0)


def dot(left, right):
    return jnp.dot(left, right, preferred_element_type=F32)


def chain_body(sizes, x_ref, w_ref, gain_ref, shift_ref, bins_ref, cot_ref,
               din_ref, dw_ref, gain_out, shift_out,
               xh, wv, wt, xt, gainv, shiftv, bins, hist, gown, dmat, dgrad, dpre, acc, small,
               wpart, wland, wsum, wgather, wide_w, gains, shifts, sland, ssum,
               load_s, own_s, store_s, hx_s, hx_r, hc_s, hc_r, wt_s, wt_r, d_s, d_r, ch_s, ch_r, pa_s, pa_r, pb_s, pb_r,
               z_s, z_r, zs_s, zs_r, y_s, y_r, ys_s, ys_r, ag_s, ag_r):
    sections, nz, ny, micro, rows, channels = sizes
    bulk = nz * ny
    ext = rows + 2 * HALO
    wide = 2 * HALO
    half = rows // SPLIT
    unit = half + 2 * HALO
    blk = 3 * channels // nz
    sub = blk // ROW_PARTS
    cols = channels // COL_PARTS
    own_count = micro // 2
    units = SPLIT * own_count
    middles = 2 * own_count
    z_order = sorted(range(1, nz), key=lambda k: -min(k, nz - k))
    y_order = sorted(range(1, ny), key=lambda k: -min(k, ny - k))
    s = lax.axis_index("section")
    b = lax.axis_index("bulk")
    c = lax.rem(s, 2)
    z = lax.rem(b, nz)
    y = b // nz
    peer = s + 1 - 2 * c
    left = lax.rem(b + bulk - 1, bulk)
    right = lax.rem(b + 1, bulk)
    first_chip = s >= sections - 2
    later_chip = s < sections - 2
    passes_on = s >= 2
    mine = own_count * c
    theirs = own_count * (1 - c)

    def z_peer(k):
        return y * nz + lax.rem(z + k, nz)

    def y_peer(k):
        return lax.rem(y + k, ny) * nz + z

    barrier = pltpu.get_barrier_semaphore()

    def greet(sec, blk_id):
        pl.semaphore_signal(barrier, inc=1, device_id=(sec, blk_id), device_id_type=MESH)

    greet(s, left)
    greet(s, right)
    greet(peer, b)

    @pl.when(passes_on)
    def _():
        greet(s - 2, b)

    @pl.when(later_chip)
    def _():
        greet(s + 2, b)

    for k in range(1, ny):
        greet(s, y_peer(k))
    for k in range(1, nz):
        greet(s, z_peer(k))

    def local(src, dst, k):
        return pltpu.make_async_copy(src, dst, load_s.at[k])

    loads = [
        local(w_ref.at[0], wv, 0),
        local(x_ref.at[0], xh.at[:, pl.ds(wide, rows)], 1),
        local(gain_ref, gainv, 2),
        local(shift_ref, shiftv, 3),
    ]
    for one in loads:
        one.start()
    cot_loads = []
    for h in range(SPLIT):
        start = max(0, half * h - HALO)
        count = min(rows, half * h + half + HALO) - start
        cot_loads.append(local(
            cot_ref.at[pl.ds(mine, own_count), pl.ds(start, count)],
            hist.at[0, :, h, pl.ds(start - half * h + HALO, count)], 4 + h))

    @pl.when(first_chip)
    def _():
        for one in cot_loads:
            one.start()

    for m in range(micro):
        bins[m] = bins_ref[m]
    loads[0].wait()
    for k in range(3):
        wt[c, k] = wv[k].astype(F32).T.astype(BF16)

    for one in loads[1:]:
        one.wait()

    def taps(xs):
        return rolled(dot(xs, wv[0]), 1) + dot(xs, wv[1]) + rolled(dot(xs, wv[2]), -1)

    def film(pre, k):
        gain = gainv[k]
        filmed = pre * gain + shiftv[k]
        sig = jax.nn.sigmoid(filmed)
        d = sig * (1.0 + filmed * (1.0 - sig))
        return d, d * gain

    def inner(j, carry):
        m = lax.rem(theirs + j, micro)
        pre = taps(xh[m, wide:wide + rows])
        d, full = film(pre, bins[m])
        dmat[c, m, HALO:HALO + rows] = full
        dgrad[m] = d
        dpre[m] = d * pre
        return carry

    lax.fori_loop(0, own_count, inner, 0)

    chain_peers = jnp.where(passes_on, 1, 0) + jnp.where(later_chip, 1, 0)
    pl.semaphore_wait(barrier, 3 + (nz - 1) + (ny - 1) + chain_peers)

    def copy(src, dst, send, recv, to):
        return pltpu.make_async_remote_copy(src_ref=src, dst_ref=dst, send_sem=send, recv_sem=recv, device_id=to, device_id_type=MESH)

    x_right = copy(x_ref.at[0, :, pl.ds(rows - wide, wide)], xh.at[:, pl.ds(0, wide)], hx_s.at[0], hx_r.at[0], (s, right))
    x_left = copy(x_ref.at[0, :, pl.ds(0, wide)], xh.at[:, pl.ds(wide + rows, wide)], hx_s.at[1], hx_r.at[1], (s, left))
    c_right = copy(cot_ref.at[pl.ds(mine, own_count), pl.ds(rows - HALO, HALO)], hist.at[0, :, 0, pl.ds(0, HALO)], hc_s.at[0], hc_r.at[0], (s, right))
    c_left = copy(cot_ref.at[pl.ds(mine, own_count), pl.ds(0, HALO)], hist.at[0, :, SPLIT - 1, pl.ds(unit - HALO, HALO)], hc_s.at[1], hc_r.at[1], (s, left))
    w_peer = copy(wt.at[c], wt.at[c], wt_s.at[0], wt_r.at[0], (peer, b))
    d_spans = (pl.ds(wide, rows - wide), pl.ds(0, wide), pl.ds(rows, wide))

    def d_copy(j, part):
        at = dmat.at[c, theirs + j, d_spans[part]]
        return copy(at, at, d_s.at[j, part], d_r.at[j, part], (peer, b))

    x_right.start()
    x_left.start()
    d_copy(0, 0).start()
    w_peer.start()
    for j in range(1, own_count):
        d_copy(j, 0).start()

    @pl.when(first_chip)
    def _():
        c_right.start()
        c_left.start()

    lax.fori_loop(own_count, micro, inner, 0)

    def outer(j, pre):
        m = lax.rem(theirs + j, micro)
        d, full = film(pre, bins[m])
        low = slice(HALO, HALO + wide)
        high = slice(2 * wide + HALO, 3 * wide + HALO)
        dmat[c, m, 0:wide] = full[low]
        dmat[c, m, rows:rows + wide] = full[high]
        if j < own_count:
            d_copy(j, 1).start()
            d_copy(j, 2).start()
        both = d * pre
        dgrad[m, 0:HALO] = d[wide:wide + HALO]
        dpre[m, 0:HALO] = both[wide:wide + HALO]
        dgrad[m, rows - HALO:rows] = d[high][0:HALO]
        dpre[m, rows - HALO:rows] = both[high][0:HALO]

    def ends_forward():
        x_right.wait_recv()
        x_left.wait_recv()
        ends = []
        for j in range(micro):
            m = lax.rem(theirs + j, micro)
            ends += [xh[m, 0:2 * wide], xh[m, rows:rows + 2 * wide]]
        pre = taps(jnp.concatenate(ends, axis=0))
        for j in range(micro):
            outer(j, pre[4 * wide * j:4 * wide * (j + 1)])

    def turn(m, carry):
        xs = xh[m].astype(F32)
        for j, sh in enumerate((1, 0, -1)):
            part = rolled(xs, sh) if sh else xs
            xt[lax.rem(m, own_count), m // own_count, j * channels:(j + 1) * channels] = part[wide:wide + rows].T.astype(BF16)
        return carry

    acc[...] = jnp.zeros_like(acc)

    def pair_term(i):
        both = []
        for k in range(2):
            m = own_count * k + i
            g = gown[m].astype(F32)
            both.append((g * dmat[c, m, HALO:HALO + rows]).astype(BF16))
            small[pl.ds(m, 1)] = jnp.sum(g * dpre[m], 0, keepdims=True)
            small[pl.ds(micro + m, 1)] = jnp.sum(g * dgrad[m], 0, keepdims=True)
        left_side = jnp.concatenate([xt[i, 0], xt[i, 1]], axis=1)
        return dot(left_side, jnp.concatenate(both, axis=0))

    def weight_pair(i):
        for k in units_of(i):
            grad_copy(k).wait_recv()
        acc[...] += pair_term(i)

    @pl.when(later_chip)
    def _():
        ends_forward()
        lax.fori_loop(0, micro, turn, 0)

    @pl.when(first_chip)
    def _():
        for one in cot_loads:
            one.wait()

    w_peer.wait_recv()

    def split(u):
        late = u // middles
        side = u % 2
        i = (u % middles) // 2
        return i, (1 - late) * (1 + side) + late * (SPLIT - 1) * side

    def units_of(i):
        return [2 * i, 2 * i + 1, middles + 2 * i, middles + 2 * i + 1]

    def chain_copy(u, whole):
        i, h = split(u)
        at = pl.ds(0, unit) if whole else pl.ds(h // 2 * HALO, unit - HALO)
        return copy(hist.at[2, i, h, at], hist.at[0, i, h, at], ch_s.at[u], ch_r.at[u], (s - 2, b))

    def side_halo(i, h):
        upper_half = h // 2
        to = (1 - upper_half) * (unit - HALO)
        source = upper_half * (h - 1) + 1 - upper_half
        start = HALO + upper_half * (half - HALO)
        hist[0, i, h, pl.ds(to, HALO)] = hist[0, i, source, pl.ds(start, HALO)]

    def spot_of(u):
        i, h = split(u)
        return mine + i, pl.ds(h * half, half)

    def grad_copy(u):
        i, h = split(u)
        m, at = spot_of(u)
        return copy(hist.at[c, i, h, pl.ds(HALO, half)], gown.at[m, at], pa_s.at[u], pa_r.at[u], (peer, b))

    def out_copy(i):
        return copy(hist.at[c + 1, i, :, pl.ds(HALO, half)], din_ref.at[mine + i], pb_s.at[i], pb_r.at[i], (peer, b))

    def own_copy(i):
        return pltpu.make_async_copy(hist.at[2 - c, i, :, pl.ds(HALO, half)], din_ref.at[mine + i], own_s.at[i])

    def back(g, sec, m, at):
        gp = (g * dmat[sec, m, at]).astype(BF16)
        out = g + dot(gp, wt[sec, 1])
        out = out + rolled(dot(gp, wt[sec, 0]), -1)
        out = out + rolled(dot(gp, wt[sec, 2]), 1)
        return out.astype(BF16)

    def chain(u):
        i, h = split(u)
        m, at = spot_of(u)
        span = pl.ds(h * half, unit)
        if u == middles - 1:
            @pl.when(first_chip)
            def _():
                ends_forward()

        if h == 1:
            d_copy(i, 0).wait_recv()
        if h == 0:
            d_copy(i, 1).wait_recv()
            d_copy(i, 2).wait_recv()
        if u == middles:
            @pl.when(first_chip)
            def _():
                c_right.wait_recv()
                c_left.wait_recv()

        @pl.when(later_chip)
        def _():
            chain_copy(u, h == 1).wait_recv()
            if h != 1:
                side_halo(i, h)

        upper = back(hist[0, i, h].astype(F32), 1, m, span)
        hist[1, i, h] = upper

        @pl.when(jnp.logical_not(passes_on))
        def _():
            grad_copy(u).start()

        lower = back(upper.astype(F32), 0, m, span)
        hist[2, i, h] = lower

        @pl.when(passes_on)
        def _():
            chain_copy(u, h == 1).start()
            grad_copy(u).start()

        if u >= middles and u % 2:
            out_copy(i).start()
            own_copy(i).start()
        gown[m, at] = hist[1 - c, i, h, HALO:HALO + half]

        k = (u - middles) // 2 - 1
        if u % 2 == 0 and 0 <= k < own_count - 1:
            @pl.when(later_chip)
            def _():
                weight_pair(k)

    for u in range(units):
        chain(u)

    @pl.when(first_chip)
    def _():
        lax.fori_loop(0, micro, turn, 0)
        for i in range(own_count - 1):
            weight_pair(i)

    for k in units_of(own_count - 1):
        grad_copy(k).wait_recv()
    last_term = pair_term(own_count - 1)

    def scatter(q, k):
        to = lax.rem(z + k, nz)
        return copy(wpart.at[q, to], wland.at[q, k], z_s.at[q, k], z_r.at[q, k], (s, y * nz + to))

    def small_z(k):
        return copy(small, sland.at[k], zs_s.at[k], zs_r.at[k], (s, z_peer(k)))

    def across(q, k):
        return copy(wsum.at[q, y], wsum.at[q, y], y_s.at[q, k], y_r.at[q, k], (s, y_peer(k)))

    def small_y(k):
        return copy(ssum.at[y], ssum.at[y], ys_s.at[k], ys_r.at[k], (s, y_peer(k)))

    def gather(q, k):
        return copy(wgather.at[q, z], wgather.at[q, z], ag_s.at[q, k], ag_r.at[q, k], (s, z_peer(k)))

    def area(q, j):
        top, side = j * blk + (q // COL_PARTS) * sub, (q % COL_PARTS) * cols
        return slice(top, top + sub), slice(side, side + cols)

    for q in range(PARTS):
        for j in range(nz):
            at_rows, at_cols = area(q, j)
            wpart[q, j] = (acc[at_rows, at_cols] + last_term[at_rows, at_cols]).astype(BF16)
        for k in z_order:
            scatter(q, k).start()
    for k in z_order:
        small_z(k).start()

    for q in range(PARTS):
        total = wpart[q, z].astype(F32)
        for k in z_order:
            scatter(q, k).wait_recv()
            total = total + wland[q, k].astype(F32)
        wsum[q, y] = total.astype(BF16)
        for k in y_order:
            across(q, k).start()

    sland[0] = small[...]
    for k in range(1, nz):
        small_z(k).wait_recv()
    tiny = sland[z]
    for j in range(1, nz):
        tiny = tiny + sland[lax.rem(z + nz - j, nz)]
    ssum[y] = tiny
    for k in y_order:
        small_y(k).start()

    for q in range(PARTS):
        for k in range(1, ny):
            across(q, k).wait_recv()
        total = wsum[q, 0].astype(F32)
        for j in range(1, ny):
            total = total + wsum[q, j].astype(F32)
        wgather[q, z] = total.astype(BF16)
        for k in z_order:
            gather(q, k).start()

    for k in range(1, ny):
        small_y(k).wait_recv()
    tiny = ssum[0]
    for j in range(1, ny):
        tiny = tiny + ssum[j]
    count = gains.shape[0]
    spot = lax.broadcasted_iota(jnp.int32, (count, 1, channels), 0)
    sum_gain = jnp.zeros((count, 1, channels), F32)
    sum_shift = jnp.zeros((count, 1, channels), F32)
    for m in range(micro):
        hit = spot == bins[m]
        sum_gain = sum_gain + jnp.where(hit, tiny[m:m + 1][None], 0.0)
        sum_shift = sum_shift + jnp.where(hit, tiny[micro + m:micro + m + 1][None], 0.0)
    gains[...] = sum_gain
    shifts[...] = sum_shift
    stores = [
        pltpu.make_async_copy(gains, gain_out, store_s.at[0]),
        pltpu.make_async_copy(shifts, shift_out, store_s.at[1]),
    ]
    for one in stores:
        one.start()

    x_right.wait_send()
    x_left.wait_send()
    w_peer.wait_send()

    @pl.when(first_chip)
    def _():
        c_right.wait_send()
        c_left.wait_send()

    for j in range(own_count):
        for part in range(3):
            d_copy(j, part).wait_send()
    for u in range(units):
        grad_copy(u).wait_send()
    for i in range(own_count):
        out_copy(i).wait()
        own_copy(i).wait()

    @pl.when(passes_on)
    def _():
        for u in range(units):
            chain_copy(u, split(u)[1] == 1).wait_send()

    for k in range(1, nz):
        small_z(k).wait_send()
    for k in range(1, ny):
        small_y(k).wait_send()
    for q in range(PARTS):
        for k in range(1, nz):
            gather(q, k).wait()
        part, side = q // COL_PARTS, q % COL_PARTS
        for j in range(nz):
            wide_w[j, part, :, side * cols:(side + 1) * cols] = wgather[q, j].astype(F32)
        if side == COL_PARTS - 1:
            stores.append(pltpu.make_async_copy(wide_w.at[:, part], dw_ref.at[:, part], store_s.at[2 + part]))
            stores[-1].start()
    for one in stores:
        one.wait()
    for q in range(PARTS):
        for k in range(1, nz):
            scatter(q, k).wait_send()
        for k in range(1, ny):
            across(q, k).wait_send()


def finish_body(din_ref, dw_ref, gain_ref, shift_ref, din_out, dw_out, gain_out, shift_out, din, dw, gains, shifts, load_s, store_s):
    micro = din_ref.shape[0]
    tap = dw_ref.shape[0] // 3
    trips = [(dw_ref.at[pl.ds(k * tap, tap)], dw.at[k], dw_out.at[0, k]) for k in range(3)]
    trips += [(din_ref.at[m], din.at[m], din_out.at[0, m]) for m in range(micro)]
    trips += [(gain_ref, gains, gain_out), (shift_ref, shifts, shift_out)]
    loads = [pltpu.make_async_copy(src, mid, load_s.at[k]) for k, (src, mid, _) in enumerate(trips)]
    stores = [pltpu.make_async_copy(mid, dst, store_s.at[k]) for k, (_, mid, dst) in enumerate(trips)]
    for one in loads:
        one.start()
    for one, two in zip(loads, stores):
        one.wait()
        two.start()
    for two in stores:
        two.wait()


def shards(sections, bulk, activations, weights, film_gain, film_shift, doa_bins, cotangent):
    micro, rows, channels = activations.shape[1:]
    bins_count = film_gain.shape[1]
    nz = 8 if bulk == 32 else 2
    ny = bulk // nz
    ext = rows + 2 * HALO
    blk = 3 * channels // nz
    sub = blk // ROW_PARTS
    cols = channels // COL_PARTS
    own = micro // 2
    units = SPLIT * own
    unit = rows // SPLIT + 2 * HALO
    sizes = (sections, nz, ny, micro, rows, channels)
    dma = pltpu.SemaphoreType.DMA
    hbm = pl.BlockSpec(memory_space=pltpu.HBM)
    smem = pl.BlockSpec(memory_space=pltpu.SMEM)
    scratch = pltpu.VMEM
    gain_rows = jnp.transpose(film_gain, (1, 0, 2))
    shift_rows = jnp.transpose(film_shift, (1, 0, 2))
    d_in, d_w, d_gain, d_shift = pl.pallas_call(
        functools.partial(chain_body, sizes),
        out_shape=(
            jax.ShapeDtypeStruct((micro, SPLIT, rows // SPLIT, channels), BF16),
            jax.ShapeDtypeStruct((nz, ROW_PARTS, sub, channels), F32),
            jax.ShapeDtypeStruct((bins_count, 1, channels), F32),
            jax.ShapeDtypeStruct((bins_count, 1, channels), F32),
        ),
        in_specs=[hbm, hbm, hbm, hbm, smem, hbm],
        out_specs=(hbm, hbm, hbm, hbm),
        scratch_shapes=[
            scratch((micro, ext + 2 * HALO, channels), BF16),
            scratch((3, channels, channels), BF16),
            scratch((2, 3, channels, channels), BF16),
            scratch((own, 2, 3 * channels, rows), BF16),
            scratch((bins_count, 1, channels), F32),
            scratch((bins_count, 1, channels), F32),
            pltpu.SMEM((micro,), jnp.int32),
            scratch((3, own, SPLIT, unit, channels), BF16),
            scratch((micro, rows, channels), BF16),
            scratch((2, micro, ext, channels), F32),
            scratch((micro, rows, channels), F32),
            scratch((micro, rows, channels), F32),
            scratch((3 * channels, channels), F32),
            scratch((2 * micro, channels), F32),
            scratch((PARTS, nz, sub, cols), BF16),
            scratch((PARTS, nz, sub, cols), BF16),
            scratch((PARTS, ny, sub, cols), BF16),
            scratch((PARTS, nz, sub, cols), BF16),
            scratch((nz, ROW_PARTS, sub, channels), F32),
            scratch((bins_count, 1, channels), F32),
            scratch((bins_count, 1, channels), F32),
            scratch((nz, 2 * micro, channels), F32),
            scratch((ny, 2 * micro, channels), F32),
            dma((4 + SPLIT,)), dma((own,)), dma((2 + ROW_PARTS,)),
            dma((2,)), dma((2,)), dma((2,)), dma((2,)), dma((1,)), dma((1,)),
            dma((own, 3)), dma((own, 3)), dma((units,)), dma((units,)),
            dma((units,)), dma((units,)), dma((own,)), dma((own,)),
            dma((PARTS, nz)), dma((PARTS, nz)), dma((nz,)), dma((nz,)),
            dma((PARTS, ny)), dma((PARTS, ny)), dma((ny,)), dma((ny,)),
            dma((PARTS, nz)), dma((PARTS, nz)),
        ],
        compiler_params=pltpu.CompilerParams(
            collective_id=0, has_side_effects=True, vmem_limit_bytes=60 * 1024 * 1024
        ),
    )(activations, weights, gain_rows, shift_rows, doa_bins, cotangent)
    d_in, d_w, d_gain, d_shift = pl.pallas_call(
        finish_body,
        out_shape=(
            jax.ShapeDtypeStruct((1, micro, rows, channels), BF16),
            jax.ShapeDtypeStruct((1, 3, channels, channels), F32),
            jax.ShapeDtypeStruct((bins_count, 1, channels), F32),
            jax.ShapeDtypeStruct((bins_count, 1, channels), F32),
        ),
        in_specs=[hbm, hbm, hbm, hbm],
        out_specs=(hbm, hbm, hbm, hbm),
        scratch_shapes=[
            scratch((micro, rows, channels), BF16),
            scratch((3, channels, channels), F32),
            scratch((bins_count, 1, channels), F32),
            scratch((bins_count, 1, channels), F32),
            dma((3 + micro + 2,)),
            dma((3 + micro + 2,)),
        ],
        compiler_params=pltpu.CompilerParams(vmem_limit_bytes=60 * 1024 * 1024),
    )(d_in.reshape(micro, rows, channels), d_w.reshape(3 * channels, channels), d_gain, d_shift)
    return (
        d_in,
        d_w,
        jnp.transpose(d_gain, (1, 0, 2)),
        jnp.transpose(d_shift, (1, 0, 2)),
    )


def solution(mesh):
    return jax.shard_map(
        functools.partial(shards, mesh.shape["section"], mesh.shape["bulk"]),
        mesh=mesh,
        in_specs=(
            P("section", None, "bulk", None),
            P("section", None, None, None),
            P("section", None, None),
            P("section", None, None),
            P(),
            P(None, "bulk", None),
        ),
        out_specs=(
            P("section", None, "bulk", None),
            P("section", None, None, None),
            P("section", None, None),
            P("section", None, None),
        ),
        check_vma=False,
    )
```

```python
import functools

import jax
import jax.numpy as jnp
from jax import lax
from jax.experimental import pallas as pl
from jax.experimental.pallas import tpu as pltpu
from jax.sharding import PartitionSpec as P

MESH = pl.DeviceIdType.MESH
F32 = jnp.float32
BF16 = jnp.bfloat16
HALO = 16
ROW_PARTS = 2
COL_PARTS = 2
PARTS = ROW_PARTS * COL_PARTS
SPLIT = 4


def rolled(value, shift):
    return pltpu.roll(value, shift % value.shape[0], 0)


def dot(left, right):
    return jnp.dot(left, right, preferred_element_type=F32)


def chain_body(sizes, x_ref, w_ref, gain_ref, shift_ref, bins_ref, cot_ref,
               din_ref, dw_ref, gain_out, shift_out,
               xh, wv, wt, xt, gainv, shiftv, bins, hist, gown, dmat, dgrad, dpre, acc, small,
               wpart, wland, wsum, wgather, gains, shifts, sland, ssum,
               load_s, own_s, store_s, hx_s, hx_r, hc_s, hc_r, wt_s, wt_r, d_s, d_r, ch_s, ch_r, pa_s, pa_r, pb_s, pb_r,
               z_s, z_r, zs_s, zs_r, y_s, y_r, ys_s, ys_r, ag_s, ag_r):
    sections, nz, ny, micro, rows, channels = sizes
    bulk = nz * ny
    ext = rows + 2 * HALO
    wide = 2 * HALO
    half = rows // SPLIT
    unit = half + 2 * HALO
    blk = 3 * channels // nz
    sub = blk // ROW_PARTS
    cols = channels // COL_PARTS
    own_count = micro // 2
    units = SPLIT * own_count
    middles = 2 * own_count
    z_order = sorted(range(1, nz), key=lambda k: -min(k, nz - k))
    y_order = sorted(range(1, ny), key=lambda k: -min(k, ny - k))
    s = lax.axis_index("section")
    b = lax.axis_index("bulk")
    c = lax.rem(s, 2)
    z = lax.rem(b, nz)
    y = b // nz
    peer = s + 1 - 2 * c
    left = lax.rem(b + bulk - 1, bulk)
    right = lax.rem(b + 1, bulk)
    first_chip = s >= sections - 2
    later_chip = s < sections - 2
    passes_on = s >= 2
    mine = own_count * c
    theirs = own_count * (1 - c)

    def z_peer(k):
        return y * nz + lax.rem(z + k, nz)

    def y_peer(k):
        return lax.rem(y + k, ny) * nz + z

    def local(src, dst, k):
        return pltpu.make_async_copy(src, dst, load_s.at[k])

    loads = [
        local(w_ref.at[0], wv, 0),
        local(x_ref.at[0], xh.at[:, pl.ds(wide, rows)], 1),
        local(gain_ref, gainv, 2),
        local(shift_ref, shiftv, 3),
    ]
    for one in loads:
        one.start()
    cot_loads = []
    for h in range(SPLIT):
        start = max(0, half * h - HALO)
        count = min(rows, half * h + half + HALO) - start
        cot_loads.append(local(
            cot_ref.at[pl.ds(mine, own_count), pl.ds(start, count)],
            hist.at[0, :, h, pl.ds(start - half * h + HALO, count)], 4 + h))

    @pl.when(first_chip)
    def _():
        for one in cot_loads:
            one.start()

    barrier = pltpu.get_barrier_semaphore()

    def greet(sec, blk_id):
        pl.semaphore_signal(barrier, inc=1, device_id=(sec, blk_id), device_id_type=MESH)

    greet(s, left)
    greet(s, right)
    greet(peer, b)

    @pl.when(passes_on)
    def _():
        greet(s - 2, b)

    @pl.when(later_chip)
    def _():
        greet(s + 2, b)

    for k in range(1, ny):
        greet(s, y_peer(k))
    for k in range(1, nz):
        greet(s, z_peer(k))

    for m in range(micro):
        bins[m] = bins_ref[m]
    loads[0].wait()
    for k in range(3):
        wt[c, k] = wv[k].astype(F32).T.astype(BF16)

    for one in loads[1:]:
        one.wait()

    def taps(xs):
        return rolled(dot(xs, wv[0]), 1) + dot(xs, wv[1]) + rolled(dot(xs, wv[2]), -1)

    def film(pre, k):
        gain = gainv[k]
        filmed = pre * gain + shiftv[k]
        sig = jax.nn.sigmoid(filmed)
        d = sig * (1.0 + filmed * (1.0 - sig))
        return d, d * gain

    def inner(j, carry):
        m = lax.rem(theirs + j, micro)
        pre = taps(xh[m, wide:wide + rows])
        d, full = film(pre, bins[m])
        dmat[c, m, HALO:HALO + rows] = full
        dgrad[m] = d
        dpre[m] = d * pre
        return carry

    lax.fori_loop(0, own_count, inner, 0)

    chain_peers = jnp.where(passes_on, 1, 0) + jnp.where(later_chip, 1, 0)
    pl.semaphore_wait(barrier, 3 + (nz - 1) + (ny - 1) + chain_peers)

    def copy(src, dst, send, recv, to):
        return pltpu.make_async_remote_copy(src_ref=src, dst_ref=dst, send_sem=send, recv_sem=recv, device_id=to, device_id_type=MESH)

    x_right = copy(x_ref.at[0, :, pl.ds(rows - wide, wide)], xh.at[:, pl.ds(0, wide)], hx_s.at[0], hx_r.at[0], (s, right))
    x_left = copy(x_ref.at[0, :, pl.ds(0, wide)], xh.at[:, pl.ds(wide + rows, wide)], hx_s.at[1], hx_r.at[1], (s, left))
    c_right = copy(cot_ref.at[pl.ds(mine, own_count), pl.ds(rows - HALO, HALO)], hist.at[0, :, 0, pl.ds(0, HALO)], hc_s.at[0], hc_r.at[0], (s, right))
    c_left = copy(cot_ref.at[pl.ds(mine, own_count), pl.ds(0, HALO)], hist.at[0, :, SPLIT - 1, pl.ds(unit - HALO, HALO)], hc_s.at[1], hc_r.at[1], (s, left))
    w_peer = copy(wt.at[c], wt.at[c], wt_s.at[0], wt_r.at[0], (peer, b))
    d_spans = (pl.ds(wide, rows - wide), pl.ds(0, wide), pl.ds(rows, wide))

    def d_copy(j, part):
        at = dmat.at[c, theirs + j, d_spans[part]]
        return copy(at, at, d_s.at[j, part], d_r.at[j, part], (peer, b))

    x_right.start()
    x_left.start()
    d_copy(0, 0).start()
    w_peer.start()
    for j in range(1, own_count):
        d_copy(j, 0).start()

    @pl.when(first_chip)
    def _():
        c_right.start()
        c_left.start()

    lax.fori_loop(own_count, micro, inner, 0)

    def outer(j, pre):
        m = lax.rem(theirs + j, micro)
        d, full = film(pre, bins[m])
        low = slice(HALO, HALO + wide)
        high = slice(2 * wide + HALO, 3 * wide + HALO)
        dmat[c, m, 0:wide] = full[low]
        dmat[c, m, rows:rows + wide] = full[high]
        if j < own_count:
            d_copy(j, 1).start()
            d_copy(j, 2).start()
        both = d * pre
        dgrad[m, 0:HALO] = d[wide:wide + HALO]
        dpre[m, 0:HALO] = both[wide:wide + HALO]
        dgrad[m, rows - HALO:rows] = d[high][0:HALO]
        dpre[m, rows - HALO:rows] = both[high][0:HALO]

    def ends_forward():
        x_right.wait_recv()
        x_left.wait_recv()
        ends = []
        for j in range(micro):
            m = lax.rem(theirs + j, micro)
            ends += [xh[m, 0:2 * wide], xh[m, rows:rows + 2 * wide]]
        pre = taps(jnp.concatenate(ends, axis=0))
        for j in range(micro):
            outer(j, pre[4 * wide * j:4 * wide * (j + 1)])

    def turn(m, carry):
        xs = xh[m].astype(F32)
        for j, sh in enumerate((1, 0, -1)):
            part = rolled(xs, sh) if sh else xs
            xt[lax.rem(m, own_count), m // own_count, j * channels:(j + 1) * channels] = part[wide:wide + rows].T.astype(BF16)
        return carry

    acc[...] = jnp.zeros_like(acc)

    def pair_term(i):
        both = []
        for k in range(2):
            m = own_count * k + i
            g = gown[m].astype(F32)
            both.append((g * dmat[c, m, HALO:HALO + rows]).astype(BF16))
            small[pl.ds(m, 1)] = jnp.sum(g * dpre[m], 0, keepdims=True)
            small[pl.ds(micro + m, 1)] = jnp.sum(g * dgrad[m], 0, keepdims=True)
        left_side = jnp.concatenate([xt[i, 0], xt[i, 1]], axis=1)
        return dot(left_side, jnp.concatenate(both, axis=0))

    def weight_pair(i):
        for k in units_of(i):
            grad_copy(k).wait_recv()
        acc[...] += pair_term(i)

    @pl.when(later_chip)
    def _():
        ends_forward()
        lax.fori_loop(0, micro, turn, 0)

    @pl.when(first_chip)
    def _():
        for one in cot_loads:
            one.wait()

    w_peer.wait_recv()

    def split(u):
        late = u // middles
        side = u % 2
        i = (u % middles) // 2
        return i, (1 - late) * (1 + side) + late * (SPLIT - 1) * side

    def units_of(i):
        return [2 * i, 2 * i + 1, middles + 2 * i, middles + 2 * i + 1]

    def chain_copy(u, whole):
        i, h = split(u)
        at = pl.ds(0, unit) if whole else pl.ds(h // 2 * HALO, unit - HALO)
        return copy(hist.at[2, i, h, at], hist.at[0, i, h, at], ch_s.at[u], ch_r.at[u], (s - 2, b))

    def side_halo(i, h):
        upper_half = h // 2
        to = (1 - upper_half) * (unit - HALO)
        source = upper_half * (h - 1) + 1 - upper_half
        start = HALO + upper_half * (half - HALO)
        hist[0, i, h, pl.ds(to, HALO)] = hist[0, i, source, pl.ds(start, HALO)]

    def spot_of(u):
        i, h = split(u)
        return mine + i, pl.ds(h * half, half)

    def grad_copy(u):
        i, h = split(u)
        m, at = spot_of(u)
        return copy(hist.at[c, i, h, pl.ds(HALO, half)], gown.at[m, at], pa_s.at[u], pa_r.at[u], (peer, b))

    def out_copy(i):
        return copy(hist.at[c + 1, i, :, pl.ds(HALO, half)], din_ref.at[mine + i], pb_s.at[i], pb_r.at[i], (peer, b))

    def own_copy(i):
        return pltpu.make_async_copy(hist.at[2 - c, i, :, pl.ds(HALO, half)], din_ref.at[mine + i], own_s.at[i])

    def back(g, sec, m, at):
        gp = (g * dmat[sec, m, at]).astype(BF16)
        out = g + dot(gp, wt[sec, 1])
        out = out + rolled(dot(gp, wt[sec, 0]), -1)
        out = out + rolled(dot(gp, wt[sec, 2]), 1)
        return out.astype(BF16)

    def chain(u):
        i, h = split(u)
        m, at = spot_of(u)
        span = pl.ds(h * half, unit)
        if u == middles - 1:
            @pl.when(first_chip)
            def _():
                ends_forward()

        if h == 1:
            d_copy(i, 0).wait_recv()
        if h == 0:
            d_copy(i, 1).wait_recv()
            d_copy(i, 2).wait_recv()
        if u == middles:
            @pl.when(first_chip)
            def _():
                c_right.wait_recv()
                c_left.wait_recv()

        @pl.when(later_chip)
        def _():
            chain_copy(u, h == 1).wait_recv()
            if h != 1:
                side_halo(i, h)

        upper = back(hist[0, i, h].astype(F32), 1, m, span)
        hist[1, i, h] = upper

        @pl.when(jnp.logical_not(passes_on))
        def _():
            grad_copy(u).start()

        lower = back(upper.astype(F32), 0, m, span)
        hist[2, i, h] = lower

        @pl.when(passes_on)
        def _():
            chain_copy(u, h == 1).start()
            grad_copy(u).start()

        if u >= middles and u % 2:
            out_copy(i).start()
            own_copy(i).start()
        gown[m, at] = hist[1 - c, i, h, HALO:HALO + half]

        k = (u - middles) // 2 - 1
        if u % 2 == 0 and 0 <= k < own_count - 1:
            @pl.when(later_chip)
            def _():
                weight_pair(k)

    for u in range(units):
        chain(u)

    @pl.when(first_chip)
    def _():
        lax.fori_loop(0, micro, turn, 0)
        for i in range(own_count - 1):
            weight_pair(i)

    for k in units_of(own_count - 1):
        grad_copy(k).wait_recv()
    last_term = pair_term(own_count - 1)

    def scatter(q, k):
        to = lax.rem(z + k, nz)
        return copy(wpart.at[q, to], wland.at[q, k], z_s.at[q, k], z_r.at[q, k], (s, y * nz + to))

    def small_z(k):
        return copy(small, sland.at[k], zs_s.at[k], zs_r.at[k], (s, z_peer(k)))

    def across(q, k):
        return copy(wsum.at[q, y], wsum.at[q, y], y_s.at[q, k], y_r.at[q, k], (s, y_peer(k)))

    def small_y(k):
        return copy(ssum.at[y], ssum.at[y], ys_s.at[k], ys_r.at[k], (s, y_peer(k)))

    def gather(q, k):
        return copy(wgather.at[q, z], wgather.at[q, z], ag_s.at[q, k], ag_r.at[q, k], (s, z_peer(k)))

    def area(q, j):
        top, side = j * blk + (q // COL_PARTS) * sub, (q % COL_PARTS) * cols
        return slice(top, top + sub), slice(side, side + cols)

    for q in range(PARTS):
        for j in range(nz):
            at_rows, at_cols = area(q, j)
            wpart[q, j] = (acc[at_rows, at_cols] + last_term[at_rows, at_cols]).astype(BF16)
        for k in z_order:
            scatter(q, k).start()
    for k in z_order:
        small_z(k).start()

    for q in range(PARTS):
        total = wpart[q, z].astype(F32)
        for k in z_order:
            scatter(q, k).wait_recv()
            total = total + wland[q, k].astype(F32)
        wsum[q, y] = total.astype(BF16)
        for k in y_order:
            across(q, k).start()

    sland[0] = small[...]
    for k in range(1, nz):
        small_z(k).wait_recv()
    tiny = sland[z]
    for j in range(1, nz):
        tiny = tiny + sland[lax.rem(z + nz - j, nz)]
    ssum[y] = tiny
    for k in y_order:
        small_y(k).start()

    for q in range(PARTS):
        for k in range(1, ny):
            across(q, k).wait_recv()
        total = wsum[q, 0].astype(F32)
        for j in range(1, ny):
            total = total + wsum[q, j].astype(F32)
        wgather[q, z] = total.astype(BF16)
        for k in z_order:
            gather(q, k).start()

    for k in range(1, ny):
        small_y(k).wait_recv()
    tiny = ssum[0]
    for j in range(1, ny):
        tiny = tiny + ssum[j]
    count = gains.shape[0]
    spot = lax.broadcasted_iota(jnp.int32, (count, 1, channels), 0)
    sum_gain = jnp.zeros((count, 1, channels), F32)
    sum_shift = jnp.zeros((count, 1, channels), F32)
    for m in range(micro):
        hit = spot == bins[m]
        sum_gain = sum_gain + jnp.where(hit, tiny[m:m + 1][None], 0.0)
        sum_shift = sum_shift + jnp.where(hit, tiny[micro + m:micro + m + 1][None], 0.0)
    gains[...] = sum_gain
    shifts[...] = sum_shift
    stores = [
        pltpu.make_async_copy(gains, gain_out, store_s.at[0]),
        pltpu.make_async_copy(shifts, shift_out, store_s.at[1]),
    ]
    for one in stores:
        one.start()

    x_right.wait_send()
    x_left.wait_send()
    w_peer.wait_send()

    @pl.when(first_chip)
    def _():
        c_right.wait_send()
        c_left.wait_send()

    for j in range(own_count):
        for part in range(3):
            d_copy(j, part).wait_send()
    for u in range(units):
        grad_copy(u).wait_send()
    for i in range(own_count):
        out_copy(i).wait()
        own_copy(i).wait()

    @pl.when(passes_on)
    def _():
        for u in range(units):
            chain_copy(u, split(u)[1] == 1).wait_send()

    for k in range(1, nz):
        small_z(k).wait_send()
    for k in range(1, ny):
        small_y(k).wait_send()
    for q in range(PARTS):
        for k in range(1, nz):
            gather(q, k).wait()
        stores.append(pltpu.make_async_copy(wgather.at[q], dw_ref.at[q], store_s.at[2 + q]))
        stores[-1].start()
    for one in stores:
        one.wait()
    for q in range(PARTS):
        for k in range(1, nz):
            scatter(q, k).wait_send()
        for k in range(1, ny):
            across(q, k).wait_send()


def finish_body(din_ref, dw_ref, gain_ref, shift_ref, din_out, dw_out, gain_out, shift_out, din, dw, wide_w, gains, shifts, load_s, store_s):
    micro = din_ref.shape[0]
    nz, cols = dw_ref.shape[1], dw_ref.shape[3]
    w_loads = [pltpu.make_async_copy(dw_ref.at[q], dw.at[q], load_s.at[q]) for q in range(PARTS)]
    w_stores = [pltpu.make_async_copy(wide_w.at[:, r], dw_out.at[:, r], store_s.at[r]) for r in range(ROW_PARTS)]
    trips = [(din_ref.at[m], din.at[m], din_out.at[0, m]) for m in range(micro)]
    trips += [(gain_ref, gains, gain_out), (shift_ref, shifts, shift_out)]
    loads = [pltpu.make_async_copy(src, mid, load_s.at[PARTS + k]) for k, (src, mid, _) in enumerate(trips)]
    stores = [pltpu.make_async_copy(mid, dst, store_s.at[ROW_PARTS + k]) for k, (_, mid, dst) in enumerate(trips)]
    for one in w_loads + loads:
        one.start()
    for q in range(PARTS):
        w_loads[q].wait()
        part, side = q // COL_PARTS, q % COL_PARTS
        for j in range(nz):
            wide_w[j, part, :, side * cols:(side + 1) * cols] = dw[q, j].astype(F32)
        if side == COL_PARTS - 1:
            w_stores[part].start()
    for one, two in zip(loads, stores):
        one.wait()
        two.start()
    for two in w_stores + stores:
        two.wait()


def shards(sections, bulk, activations, weights, film_gain, film_shift, doa_bins, cotangent):
    micro, rows, channels = activations.shape[1:]
    bins_count = film_gain.shape[1]
    nz = 8 if bulk == 32 else 2
    ny = bulk // nz
    ext = rows + 2 * HALO
    blk = 3 * channels // nz
    sub = blk // ROW_PARTS
    cols = channels // COL_PARTS
    own = micro // 2
    units = SPLIT * own
    unit = rows // SPLIT + 2 * HALO
    sizes = (sections, nz, ny, micro, rows, channels)
    dma = pltpu.SemaphoreType.DMA
    hbm = pl.BlockSpec(memory_space=pltpu.HBM)
    smem = pl.BlockSpec(memory_space=pltpu.SMEM)
    scratch = pltpu.VMEM
    gain_rows = jnp.transpose(film_gain, (1, 0, 2))
    shift_rows = jnp.transpose(film_shift, (1, 0, 2))
    d_in, d_w, d_gain, d_shift = pl.pallas_call(
        functools.partial(chain_body, sizes),
        out_shape=(
            jax.ShapeDtypeStruct((micro, SPLIT, rows // SPLIT, channels), BF16),
            jax.ShapeDtypeStruct((PARTS, nz, sub, cols), BF16),
            jax.ShapeDtypeStruct((bins_count, 1, channels), F32),
            jax.ShapeDtypeStruct((bins_count, 1, channels), F32),
        ),
        in_specs=[hbm, hbm, hbm, hbm, smem, hbm],
        out_specs=(hbm, hbm, hbm, hbm),
        scratch_shapes=[
            scratch((micro, ext + 2 * HALO, channels), BF16),
            scratch((3, channels, channels), BF16),
            scratch((2, 3, channels, channels), BF16),
            scratch((own, 2, 3 * channels, rows), BF16),
            scratch((bins_count, 1, channels), F32),
            scratch((bins_count, 1, channels), F32),
            pltpu.SMEM((micro,), jnp.int32),
            scratch((3, own, SPLIT, unit, channels), BF16),
            scratch((micro, rows, channels), BF16),
            scratch((2, micro, ext, channels), F32),
            scratch((micro, rows, channels), F32),
            scratch((micro, rows, channels), F32),
            scratch((3 * channels, channels), F32),
            scratch((2 * micro, channels), F32),
            scratch((PARTS, nz, sub, cols), BF16),
            scratch((PARTS, nz, sub, cols), BF16),
            scratch((PARTS, ny, sub, cols), BF16),
            scratch((PARTS, nz, sub, cols), BF16),
            scratch((bins_count, 1, channels), F32),
            scratch((bins_count, 1, channels), F32),
            scratch((nz, 2 * micro, channels), F32),
            scratch((ny, 2 * micro, channels), F32),
            dma((4 + SPLIT,)), dma((own,)), dma((2 + PARTS,)),
            dma((2,)), dma((2,)), dma((2,)), dma((2,)), dma((1,)), dma((1,)),
            dma((own, 3)), dma((own, 3)), dma((units,)), dma((units,)),
            dma((units,)), dma((units,)), dma((own,)), dma((own,)),
            dma((PARTS, nz)), dma((PARTS, nz)), dma((nz,)), dma((nz,)),
            dma((PARTS, ny)), dma((PARTS, ny)), dma((ny,)), dma((ny,)),
            dma((PARTS, nz)), dma((PARTS, nz)),
        ],
        compiler_params=pltpu.CompilerParams(
            collective_id=0, has_side_effects=True, vmem_limit_bytes=60 * 1024 * 1024
        ),
    )(activations, weights, gain_rows, shift_rows, doa_bins, cotangent)
    d_in, d_w, d_gain, d_shift = pl.pallas_call(
        finish_body,
        out_shape=(
            jax.ShapeDtypeStruct((1, micro, rows, channels), BF16),
            jax.ShapeDtypeStruct((nz, ROW_PARTS, sub, channels), F32),
            jax.ShapeDtypeStruct((bins_count, 1, channels), F32),
            jax.ShapeDtypeStruct((bins_count, 1, channels), F32),
        ),
        in_specs=[hbm, hbm, hbm, hbm],
        out_specs=(hbm, hbm, hbm, hbm),
        scratch_shapes=[
            scratch((micro, rows, channels), BF16),
            scratch((PARTS, nz, sub, cols), BF16),
            scratch((nz, ROW_PARTS, sub, channels), F32),
            scratch((bins_count, 1, channels), F32),
            scratch((bins_count, 1, channels), F32),
            dma((PARTS + micro + 2,)),
            dma((ROW_PARTS + micro + 2,)),
        ],
        compiler_params=pltpu.CompilerParams(vmem_limit_bytes=60 * 1024 * 1024),
    )(d_in.reshape(micro, rows, channels), d_w, d_gain, d_shift)
    return (
        d_in,
        d_w.reshape(1, 3, channels, channels),
        jnp.transpose(d_gain, (1, 0, 2)),
        jnp.transpose(d_shift, (1, 0, 2)),
    )


def solution(mesh):
    return jax.shard_map(
        functools.partial(shards, mesh.shape["section"], mesh.shape["bulk"]),
        mesh=mesh,
        in_specs=(
            P("section", None, "bulk", None),
            P("section", None, None, None),
            P("section", None, None),
            P("section", None, None),
            P(),
            P(None, "bulk", None),
        ),
        out_specs=(
            P("section", None, "bulk", None),
            P("section", None, None, None),
            P("section", None, None),
            P("section", None, None),
        ),
        check_vma=False,
    )
```
